128 devices in a mesh: dp: 64 (over x_lo, z, y, core), tensor: 2 (over x_hi).
Axes of the slice: x: 4 (x_hi: 2, x_lo: 2; x = x_hi * 2 + x_lo), y: 4, z: 4, core: 2. Of those that a mesh axis runs over, the one named last changes fastest.
Arguments:
- tokens: bfloat16 [64, 512, 768], P('dp', 'tensor'), may hold values from -6 to 6
- doc_lengths: int32 [64, 2], P('dp'), may hold values from 0 to 512, as said below
- qkv_weight: bfloat16 [2, 3, 768, 768], P(None, None, 'tensor', 'dp'), may hold values from -0.21875 to 0.21875
- out_weight: bfloat16 [2, 768, 768], P(None, 'tensor', 'dp'), may hold values from -0.875 to 0.875
- inner_weight: bfloat16 [2, 3072, 768], P(None, 'tensor', 'dp'), may hold values from -0.21875 to 0.21875
- down_weight: bfloat16 [2, 3072, 768], P(None, 'tensor', 'dp'), may hold values from -0.109375 to 0.109375
- query_value_bias: float32 [2, 2, 768], P(None, None, 'tensor'), may hold values from -3 to 3
- hidden_bias: float32 [2, 3072], P(None, 'tensor'), may hold values from -3 to 3
- shifts: float32 [2, 4, 768], replicated, may hold values from -3 to 3
- gains: float32 [2, 2, 768], replicated, may hold values from 0.1 to 1.9
- cotangent: float32 [64, 512, 768], P('dp', 'tensor'), may hold values from -6 to 6
Outputs:
- output: float32 [64, 512, 768], P('dp', 'tensor')
- input_grad: float32 [64, 512, 768], P('dp', 'tensor')
- qkv_weight_grad: float32 [2, 3, 768, 768], P(None, None, 'tensor', 'dp')
- out_weight_grad: float32 [2, 768, 768], P(None, 'tensor', 'dp')
- inner_weight_grad: float32 [2, 3072, 768], P(None, 'tensor', 'dp')
- down_weight_grad: float32 [2, 3072, 768], P(None, 'tensor', 'dp')
- query_value_bias_grad: float32 [2, 2, 768], P(None, None, 'tensor')
- hidden_bias_grad: float32 [2, 3072], P(None, 'tensor')
- shift_grad: float32 [2, 4, 768], replicated
- gain_grad: float32 [2, 2, 768], replicated
The draws below stay inside these ranges and needn't reach their ends.
Inputs may be any that keep to these rules, and one draw needn't show every extreme that they name: `doc_lengths`: each row holds a first document of more than 256 positions from its start, then a second one of 64 positions or more, or none, then padding; in every draw one row is a single document that fills it.
All inputs are finite; a program needn't handle non-finite values.
Results may differ from the reference program's by a relative error of at most 0.02.
Values may be sent and summed in bfloat16 or wider, within the bound.
No kernel may reach another device: no remote copies, remote signals or barrier semaphores. Data moves between devices by JAX's collectives and lax.ppermute only.
A program may use at most 192 MiB of HBM per device.

```python
import math
import jax
import jax.numpy as jnp
from jax import lax

D = 768
HEADS = 12
HEAD = 64
FF = 3072
LAYERS = 2
ROW_LEN = 512
ROWS = 64


def draw_doc_lengths(key, part):
    key = jax.random.fold_in(key, 7)
    first_key, second_key, full_key = jax.random.split(key, 3)
    first_len = jax.random.randint(first_key, (ROWS,), ROW_LEN // 2 + 1, ROW_LEN * 7 // 8 + 1)
    least_len = ROW_LEN // 8
    spare_room = ROW_LEN - first_len - least_len + 1
    second_len = least_len + jax.random.randint(second_key, (ROWS,), 0, ROW_LEN) % spare_room
    full_row = jax.random.randint(full_key, (), 0, ROWS)
    row_index = jnp.arange(ROWS)
    first_len = jnp.where(row_index == full_row, ROW_LEN, first_len)
    second_len = jnp.where(row_index == full_row, 0, second_len)
    return jnp.stack([first_len, second_len], axis=1).astype(jnp.int32)


def block_levels(stream_key, dims, cuts, low, largest):
    factor_of, own = 1.0, jax.random.fold_in(stream_key, 6)
    for dim, parts in cuts:
        draws = jnp.exp(jax.random.uniform(jax.random.fold_in(own, dim), (parts,), jnp.float32, low / len(cuts), largest / len(cuts)))
        factor_of = factor_of * jnp.repeat(draws, dims[dim] // parts).reshape([-1 if axis == dim else 1 for axis in range(len(dims))])
    return factor_of


def bell_draw(stream_key, dims, scale, most, pieces=(), kind=jnp.bfloat16):
    entries = jax.random.normal(stream_key, dims, jnp.float32) * scale
    if len(pieces) > 0:
        entries = block_levels(stream_key, dims, pieces, -0.22, 0.18) * entries
    return jnp.clip(entries, min=-most, max=most).astype(kind)


def setup_inputs(seed: int = 0) -> dict:
    key_of = jax.random.split(jax.random.key(seed), 12)
    return {
        "tokens": bell_draw(key_of[0], (ROWS, ROW_LEN, D), 1.0, 6.0, ((0, 64), (1, 2))),
        "doc_lengths": draw_doc_lengths(jax.random.fold_in(key_of[11], 71), 0),
        "qkv_weight": bell_draw(key_of[2], (LAYERS, 3, D, D), D ** -0.5, 0.21875, ((2, 2), (3, 64))),
        "out_weight": bell_draw(key_of[3], (LAYERS, D, D), (D // 16) ** -0.5, 0.875, ((1, 2), (2, 64))),
        "inner_weight": bell_draw(key_of[4], (LAYERS, FF, D), D ** -0.5, 0.21875, ((1, 2), (2, 64))),
        "down_weight": bell_draw(key_of[5], (LAYERS, FF, D), FF ** -0.5, 0.109375, ((1, 2), (2, 64))),
        "query_value_bias": bell_draw(key_of[6], (LAYERS, 2, D), 0.5, 3.0, ((2, 2),), jnp.float32),
        "hidden_bias": bell_draw(key_of[7], (LAYERS, FF), 0.5, 3.0, ((1, 2),), jnp.float32),
        "shifts": bell_draw(key_of[8], (LAYERS, 4, D), 0.5, 3.0, (), jnp.float32),
        "gains": jnp.clip(1.0 + 0.18 * jax.random.normal(key_of[9], (LAYERS, 2, D), jnp.float32), 0.1, 1.9),
        "cotangent": bell_draw(key_of[10], (ROWS, ROW_LEN, D), 1.0, 6.0, ((0, 64), (1, 2)), jnp.float32),
    }


@jax.custom_vjp
def low(v):
    return lax.optimization_barrier(v.astype(jnp.bfloat16)).astype(jnp.float32)

@jax.custom_vjp
def low_back(v):
    return v

def low_keep(v):
    return (low(v), None)

def low_pass(kept, grad):
    return (grad,)

def back_keep(v):
    return (v, None)

def back_low(kept, grad):
    return (low(grad),)
low.defvjp(low_keep, low_pass)
low_back.defvjp(back_keep, back_low)
epsilon = 1e-06
masked_value = -1e+30
highest = lax.Precision.HIGHEST

def layer_norm(values, gain_vec, shift_vec):
    center = values - lax.optimization_barrier(jnp.mean(values, axis=-1, keepdims=True))
    variance = lax.optimization_barrier(jnp.mean(center * center, axis=-1, keepdims=True))
    return center * lax.rsqrt(variance + epsilon) * gain_vec + shift_vec

def segment_ids(doc_lengths, row_len):
    position = jnp.arange(row_len, dtype=jnp.int32)[None, :]
    first_end = doc_lengths[:, 0:1].astype(jnp.int32)
    second_end = first_end + doc_lengths[:, 1:2].astype(jnp.int32)
    return (position >= first_end).astype(jnp.int32) + (position >= second_end).astype(jnp.int32)

def attend_row(packed):
    queries, keys_all, values_all, segment = packed
    scores = jnp.einsum('hqd,hkd->hqk', queries, keys_all, precision=highest) * (1.0 / math.sqrt(HEAD))
    scores = low_back(scores)
    same_doc = segment[:, None] == segment[None, :]
    scores = jnp.where(same_doc[None], scores, masked_value)
    row_max = lax.optimization_barrier(jnp.max(scores, axis=-1, keepdims=True))
    raised = jnp.exp(scores - row_max)
    attn_probs = low(raised / lax.optimization_barrier(jnp.sum(raised, axis=-1, keepdims=True)))
    return jnp.einsum('hqk,hkd->hqd', attn_probs, values_all, precision=highest)

def split_heads(matrix, row_count):
    return matrix.reshape(row_count, ROW_LEN, HEADS, HEAD).transpose(0, 2, 1, 3)

def forward(hidden_in, qkv_weight, out_weight, inner_weight, down_weight, query_value_bias, hidden_bias, shifts, gains, segment):
    row_count = hidden_in.shape[0]
    hidden_state = hidden_in
    for layer_idx in range(LAYERS):
        rounded = low(hidden_state)
        projected = jnp.einsum('rtd,ced->crte', rounded, qkv_weight[layer_idx], precision=highest)
        queries = low(low_back(projected[0] + query_value_bias[layer_idx, 0]))
        keys_all = low(low_back(projected[1]))
        values_all = low(low_back(projected[2] + query_value_bias[layer_idx, 1]))
        attended = lax.map(jax.checkpoint(attend_row), (split_heads(queries, row_count), split_heads(keys_all, row_count), split_heads(values_all, row_count), segment))
        merged = attended.transpose(0, 2, 1, 3).reshape(row_count, ROW_LEN, D)
        merged = low(low_back(merged))
        branch = low_back(jnp.einsum('rti,io->rto', merged, out_weight[layer_idx], precision=highest))
        normed = layer_norm(hidden_state + branch + shifts[layer_idx, 0], gains[layer_idx, 0], shifts[layer_idx, 1])
        normed_low = low(normed)
        pre_act = low_back(jnp.einsum('rtd,fd->rtf', normed_low, inner_weight[layer_idx], precision=highest) + hidden_bias[layer_idx])
        activated = low(jax.nn.gelu(pre_act, approximate=False))
        mlp_out = low_back(jnp.einsum('rtf,fd->rtd', activated, down_weight[layer_idx], precision=highest))
        hidden_state = layer_norm(normed + mlp_out + shifts[layer_idx, 2], gains[layer_idx, 1], shifts[layer_idx, 3])
    return hidden_state

def reference(tokens, doc_lengths, qkv_weight, out_weight, inner_weight, down_weight, query_value_bias, hidden_bias, shifts, gains, cotangent):
    segment = segment_ids(doc_lengths, ROW_LEN)

    def run_layers(hidden_in, qkv_f, out_f, inner_f, down_f, bias_qv, bias_hidden, shift_f, gain_f):
        return forward(hidden_in, qkv_f, out_f, inner_f, down_f, bias_qv, bias_hidden, shift_f, gain_f, segment)
    output, pull_back = jax.vjp(run_layers, tokens.astype(jnp.float32), qkv_weight.astype(jnp.float32), out_weight.astype(jnp.float32), inner_weight.astype(jnp.float32), down_weight.astype(jnp.float32), query_value_bias.astype(jnp.float32), hidden_bias.astype(jnp.float32), shifts.astype(jnp.float32), gains.astype(jnp.float32))
    all_grads = pull_back(cotangent.astype(jnp.float32))
    return (output, all_grads[0], all_grads[1], all_grads[2], all_grads[3], all_grads[4], all_grads[5], all_grads[6], all_grads[7], all_grads[8])
```

```python
import math

import jax
import jax.numpy as jnp
from jax import lax
from jax.sharding import PartitionSpec as P

HEAD = 64
LAYERS = 2
ALL = ("tensor", "dp")


epsilon = 1e-06
masked_value = -1e30


def layer_norm(values, gain_vec, shift_vec):
    center = values - jnp.mean(values, axis=-1, keepdims=True)
    variance = jnp.mean(center * center, axis=-1, keepdims=True)
    inverse = lax.rsqrt(variance + epsilon)
    normal = center * inverse
    return normal * gain_vec + shift_vec, normal, inverse


def norm_back(grad, normal, inverse, gain_vec):
    scaled = grad * gain_vec
    mean_one = jnp.mean(scaled, axis=-1, keepdims=True)
    mean_two = jnp.mean(scaled * normal, axis=-1, keepdims=True)
    return inverse * (scaled - mean_one - normal * mean_two)


def exact_gelu(values):
    return jax.nn.gelu(values, approximate=False)


def nn(left, right):
    return lax.dot_general(left, right, (((1,), (0,)), ((), ())), preferred_element_type=jnp.float32)


def nt(left, right):
    return lax.dot_general(left, right, (((1,), (1,)), ((), ())), preferred_element_type=jnp.float32)


def tn(left, right):
    return lax.dot_general(left, right, (((0,), (0,)), ((), ())), preferred_element_type=jnp.float32)


def swap_halves(values):
    return lax.ppermute(values, "tensor", [(0, 1), (1, 0)])


def gather_weights(qkv_weight, out_weight, inner_weight, down_weight):
    layers = qkv_weight.shape[0]
    thin = qkv_weight.shape[3]
    piece = jnp.concatenate(
        [qkv_weight.reshape(layers, -1, thin), out_weight, inner_weight, down_weight], axis=1
    )
    width = piece.shape[1]
    piece = piece.transpose(0, 2, 1).reshape(layers * thin, width)
    whole = lax.all_gather(piece, ALL, axis=0, tiled=True)
    whole = whole.reshape(2, -1, layers, thin, width)
    return [whole[:, :, layer].reshape(2, -1, width) for layer in range(layers)]


def split_heads(matrix):
    return matrix.reshape(matrix.shape[0], -1, HEAD).transpose(1, 0, 2)


def join_heads(matrix):
    return matrix.transpose(1, 0, 2).reshape(matrix.shape[1], -1)


def body(
    tokens,
    doc_lengths,
    qkv_weight,
    out_weight,
    inner_weight,
    down_weight,
    query_value_bias,
    hidden_bias,
    shifts,
    gains,
    cotangent,
):
    half_len, features = tokens.shape[1:]
    thin = qkv_weight.shape[3]
    head_cols = qkv_weight.shape[2]
    hidden_cols = inner_weight.shape[1]
    scale_factor = 1.0 / math.sqrt(HEAD)
    tensor_idx = lax.axis_index("tensor")
    dp_idx = lax.axis_index("dp")

    weights = gather_weights(qkv_weight, out_weight, inner_weight, down_weight)
    bias_rows = jnp.concatenate(
        [query_value_bias.reshape(2 * LAYERS, head_cols), hidden_bias.reshape(-1, head_cols)], axis=0
    )
    bias_all = lax.all_gather(bias_rows, "tensor", axis=0, tiled=False)
    qv_bias = bias_all[:, : 2 * LAYERS].reshape(2, LAYERS, 2, head_cols)
    qv_bias = qv_bias.transpose(1, 2, 0, 3).reshape(LAYERS, 2, 2 * head_cols)
    hidden_full = bias_all[:, 2 * LAYERS :].reshape(2, LAYERS, hidden_cols)
    hidden_full = hidden_full.transpose(1, 0, 2).reshape(LAYERS, 2 * hidden_cols)

    position = jnp.arange(half_len, dtype=jnp.int32)
    mine_pos = position + tensor_idx * half_len
    key_pos = jnp.concatenate([mine_pos, position + (1 - tensor_idx) * half_len])
    first_end = doc_lengths[0, 0]
    second_end = first_end + doc_lengths[0, 1]

    def segment(pos):
        return (pos >= first_end).astype(jnp.int32) + (pos >= second_end).astype(jnp.int32)

    same_doc = segment(mine_pos)[:, None] == segment(key_pos)[None, :]

    cut = [0, head_cols, 2 * head_cols, 3 * head_cols, 4 * head_cols, 4 * head_cols + hidden_cols, 4 * head_cols + 2 * hidden_cols]

    def section(layer_idx, which, part):
        return weights[layer_idx][part, :, cut[which] : cut[which + 1]]

    def project(values, layer_idx, which):
        return jnp.concatenate([nn(values, section(layer_idx, which, p)) for p in range(2)], axis=1)

    def project_back(values, layer_idx, which):
        width = values.shape[1] // 2
        return nt(values[:, :width], section(layer_idx, which, 0)) + nt(
            values[:, width:], section(layer_idx, which, 1)
        )

    hidden_state = tokens[0].astype(jnp.float32)
    rounded = tokens[0]
    saved_acts = []
    for layer_idx in range(LAYERS):
        rows = jnp.concatenate([rounded, swap_halves(rounded)], axis=0)
        query_b = (project(rounded, layer_idx, 0) + qv_bias[layer_idx, 0]).astype(jnp.bfloat16)
        key_b = project(rows, layer_idx, 1).astype(jnp.bfloat16)
        value_b = (project(rows, layer_idx, 2) + qv_bias[layer_idx, 1]).astype(jnp.bfloat16)
        query_h, key_h, value_h = split_heads(query_b), split_heads(key_b), split_heads(value_b)
        scores = (
            jnp.einsum("hqd,hkd->hqk", query_h, key_h, preferred_element_type=jnp.float32) * scale_factor
        )
        scores = jnp.where(same_doc[None], scores, masked_value)
        row_max = jnp.max(scores, axis=-1, keepdims=True)
        raised = jnp.exp(scores - row_max)
        row_total = jnp.sum(raised, axis=-1, keepdims=True)
        attn_probs = (raised / row_total).astype(jnp.bfloat16)
        log_total = row_max + jnp.log(row_total)
        attended = jnp.einsum("hqk,hkd->hqd", attn_probs, value_h, preferred_element_type=jnp.float32)
        attended_b = join_heads(attended.astype(jnp.bfloat16))
        branch = project_back(attended_b, layer_idx, 3)
        normed, normal_one, inverse_one = layer_norm(
            hidden_state + branch + shifts[layer_idx, 0], gains[layer_idx, 0], shifts[layer_idx, 1]
        )
        normed_low = normed.astype(jnp.bfloat16)
        pre_act = project(normed_low, layer_idx, 4) + hidden_full[layer_idx]
        activated_b = exact_gelu(pre_act).astype(jnp.bfloat16)
        mlp_out = project_back(activated_b, layer_idx, 5)
        hidden_state, normal_two, inverse_two = layer_norm(
            normed + mlp_out + shifts[layer_idx, 2], gains[layer_idx, 1], shifts[layer_idx, 3]
        )
        saved_acts.append(
            (rows, query_h, key_h, value_h, log_total, attended_b, normal_one, inverse_one, normed_low,
             pre_act, activated_b, normal_two, inverse_two)
        )
        rounded = hidden_state.astype(jnp.bfloat16)
    output = hidden_state

    state_grad = cotangent[0]
    weight_parts = [None] * LAYERS
    small_parts = [None] * LAYERS
    for layer_idx in reversed(range(LAYERS)):
        (rows, query_h, key_h, value_h, log_total, attended_b, normal_one, inverse_one, normed_low,
         pre_act, activated_b, normal_two, inverse_two) = saved_acts[layer_idx]
        pre_two_grad = norm_back(state_grad, normal_two, inverse_two, gains[layer_idx, 1])
        gain_two = jnp.sum(state_grad * normal_two, axis=0)
        beta_two = jnp.sum(state_grad, axis=0)
        shift_two = jnp.sum(pre_two_grad, axis=0)
        mlp_grad_b = pre_two_grad.astype(jnp.bfloat16)
        down_local = tn(mlp_grad_b, activated_b).astype(jnp.bfloat16)
        activated_grad = project(mlp_grad_b, layer_idx, 5)
        _, gelu_back = jax.vjp(exact_gelu, pre_act)
        pre_act_grad = gelu_back(activated_grad)[0].astype(jnp.bfloat16)
        hidden_part = jnp.sum(pre_act_grad.astype(jnp.float32), axis=0)
        inner_local = tn(normed_low, pre_act_grad).astype(jnp.bfloat16)
        normed_grad = pre_two_grad + project_back(pre_act_grad, layer_idx, 4)
        pre_one_grad = norm_back(normed_grad, normal_one, inverse_one, gains[layer_idx, 0])
        gain_one = jnp.sum(normed_grad * normal_one, axis=0)
        beta_one = jnp.sum(normed_grad, axis=0)
        shift_one = jnp.sum(pre_one_grad, axis=0)
        attn_grad_b = pre_one_grad.astype(jnp.bfloat16)
        out_local = tn(attn_grad_b, attended_b).astype(jnp.bfloat16)
        attended_grad = project(attn_grad_b, layer_idx, 3).astype(jnp.bfloat16)
        attended_grad_h = split_heads(attended_grad)
        scores = (
            jnp.einsum("hqd,hkd->hqk", query_h, key_h, preferred_element_type=jnp.float32) * scale_factor
        )
        scores = jnp.where(same_doc[None], scores, masked_value)
        probs_full = jnp.exp(scores - log_total)
        probs_low = probs_full.astype(jnp.bfloat16)
        value_grad = jnp.einsum("hqk,hqd->hkd", probs_low, attended_grad_h, preferred_element_type=jnp.float32)
        prob_grad = jnp.einsum("hqd,hkd->hqk", attended_grad_h, value_h, preferred_element_type=jnp.float32)
        row_dot = jnp.sum(prob_grad * probs_full, axis=-1, keepdims=True)
        score_grad = (probs_full * (prob_grad - row_dot)).astype(jnp.bfloat16)
        query_grad = (
            jnp.einsum("hqk,hkd->hqd", score_grad, key_h, preferred_element_type=jnp.float32) * scale_factor
        )
        key_grad = (
            jnp.einsum("hqk,hqd->hkd", score_grad, query_h, preferred_element_type=jnp.float32) * scale_factor
        )
        query_grad_b = join_heads(query_grad.astype(jnp.bfloat16))
        key_grad_b = join_heads(key_grad.astype(jnp.bfloat16))
        value_grad_b = join_heads(value_grad.astype(jnp.bfloat16))
        qv_part = jnp.concatenate(
            [
                jnp.sum(query_grad_b.astype(jnp.float32), axis=0),
                jnp.sum(value_grad_b.astype(jnp.float32), axis=0),
            ]
        )
        query_local = tn(rows[:half_len], query_grad_b).astype(jnp.bfloat16)
        key_local = tn(rows, key_grad_b).astype(jnp.bfloat16)
        value_local = tn(rows, value_grad_b).astype(jnp.bfloat16)
        both = project_back(key_grad_b, layer_idx, 1) + project_back(value_grad_b, layer_idx, 2)
        theirs = swap_halves(both[half_len:].astype(jnp.bfloat16))
        state_grad = (
            pre_one_grad
            + project_back(query_grad_b, layer_idx, 0)
            + both[:half_len]
            + theirs.astype(jnp.float32)
        )
        weight_parts[layer_idx] = (query_local, key_local, value_local, out_local, inner_local, down_local)
        small_parts[layer_idx] = jnp.concatenate(
            [shift_one, beta_one, shift_two, beta_two, gain_one, gain_two, qv_part, hidden_part]
        )
    small = jnp.stack(small_parts).reshape(-1, 2 * hidden_cols).astype(jnp.bfloat16)
    small_rows = small.shape[0]
    small = jnp.pad(small, ((0, -small_rows % 16), (0, 0)))
    with_small = jnp.concatenate([weight_parts[0][5], small], axis=0)
    summed = lax.optimization_barrier(lax.psum((*weight_parts[0][:5], with_small, *weight_parts[1]), ALL))
    small_sum = summed[5][features : features + small_rows].astype(jnp.float32).reshape(LAYERS, -1)
    shift_total = small_sum[:, : 4 * features].reshape(LAYERS, 4, features)
    gain_total = small_sum[:, 4 * features : 6 * features].reshape(LAYERS, 2, features)
    qv_total = lax.dynamic_slice_in_dim(
        small_sum[:, 6 * features : 8 * features].reshape(LAYERS, 2, features), tensor_idx * head_cols, head_cols, 2
    )
    hidden_total = lax.dynamic_slice_in_dim(small_sum[:, 8 * features :], tensor_idx * hidden_cols, hidden_cols, 1)

    def own(layer_idx, which):
        array = summed[6 * layer_idx + which]
        width = array.shape[1] // 2
        part = lax.dynamic_slice(array, (dp_idx * thin, tensor_idx * width), (thin, width))
        return part.astype(jnp.float32).T

    qkv_result = jnp.stack([jnp.stack([own(l, w) for w in range(3)]) for l in range(LAYERS)])
    out_result, inner_result, down_result = (
        jnp.stack([own(l, w) for l in range(LAYERS)]) for w in (3, 4, 5)
    )
    return (
        output[None],
        state_grad[None],
        qkv_result,
        out_result,
        inner_result,
        down_result,
        qv_total,
        hidden_total,
        shift_total,
        gain_total,
    )


def solution(mesh):
    in_specs = (
        P("dp", "tensor", None),
        P("dp", None),
        P(None, None, "tensor", "dp"),
        P(None, "tensor", "dp"),
        P(None, "tensor", "dp"),
        P(None, "tensor", "dp"),
        P(None, None, "tensor"),
        P(None, "tensor"),
        P(),
        P(),
        P("dp", "tensor", None),
    )
    out_specs = (
        P("dp", "tensor", None),
        P("dp", "tensor", None),
        P(None, None, "tensor", "dp"),
        P(None, "tensor", "dp"),
        P(None, "tensor", "dp"),
        P(None, "tensor", "dp"),
        P(None, None, "tensor"),
        P(None, "tensor"),
        P(),
        P(),
    )
    return jax.shard_map(body, mesh=mesh, in_specs=in_specs, out_specs=out_specs, check_vma=False)
```

```python
import math

import jax
import jax.numpy as jnp
from jax import lax
from jax.experimental import pallas as pl
from jax.experimental.pallas import tpu as pltpu
from jax.sharding import PartitionSpec as P

HEAD = 64
LAYERS = 2
ALL = ("tensor", "dp")


epsilon = 1e-06
masked_value = -1e30


def layer_norm(values, gain_vec, shift_vec):
    center = values - jnp.mean(values, axis=-1, keepdims=True)
    variance = jnp.mean(center * center, axis=-1, keepdims=True)
    inverse = lax.rsqrt(variance + epsilon)
    normal = center * inverse
    return normal * gain_vec + shift_vec, normal, inverse


def norm_back(grad, normal, inverse, gain_vec):
    scaled = grad * gain_vec
    mean_one = jnp.mean(scaled, axis=-1, keepdims=True)
    mean_two = jnp.mean(scaled * normal, axis=-1, keepdims=True)
    return inverse * (scaled - mean_one - normal * mean_two)


def exact_gelu(values):
    return jax.nn.gelu(values, approximate=False)


def nn(left, right):
    return lax.dot_general(left, right, (((1,), (0,)), ((), ())), preferred_element_type=jnp.float32)


def nt(left, right):
    return lax.dot_general(left, right, (((1,), (1,)), ((), ())), preferred_element_type=jnp.float32)


def tn(left, right):
    return lax.dot_general(left, right, (((0,), (0,)), ((), ())), preferred_element_type=jnp.float32)


def swap_halves(values):
    return lax.ppermute(values, "tensor", [(0, 1), (1, 0)])


def unpack_kernel(order_ref, packed_ref, query_ref, key_value_ref, out_ref, inner_ref, down_ref):
    picked = jnp.dot(order_ref[...], packed_ref[...], preferred_element_type=jnp.float32)
    picked = picked.astype(jnp.bfloat16)
    rows, cols = query_ref.shape
    hidden = inner_ref.shape[1] // 2
    query_ref[...] = picked[:rows, :cols]
    key_value_ref[0] = picked[:rows, cols : 2 * cols]
    key_value_ref[1] = picked[:rows, 2 * cols : 3 * cols]
    out_ref[...] = picked[:rows, 3 * cols : 4 * cols]
    inner_ref[:, :hidden] = picked[:rows, 4 * cols :]
    inner_ref[:, hidden:] = picked[rows:, :hidden]
    down_ref[...] = picked[rows:, hidden:]


def unpack_layer(gathered, layer_idx, thin, features, cols, hidden):
    group = 8
    tall = 2 * thin * group
    flat = thin * group
    width = gathered.shape[1] // LAYERS
    blocks = features // flat
    spot = jnp.arange(tall, dtype=jnp.int32)
    half = spot // flat
    source = (spot % flat) // thin * (2 * thin) + half * thin + spot % thin
    order = (source[:, None] == jnp.arange(tall, dtype=jnp.int32)[None, :]).astype(jnp.bfloat16)
    return pl.pallas_call(
        unpack_kernel,
        grid=(2, blocks),
        in_specs=[
            pl.BlockSpec((tall, tall), lambda t, r: (0, 0)),
            pl.BlockSpec((tall, width), lambda t, r: (t * blocks + r, layer_idx)),
        ],
        out_specs=[
            pl.BlockSpec((flat, cols), lambda t, r: (r, t)),
            pl.BlockSpec((2, flat, cols), lambda t, r: (0, r, t)),
            pl.BlockSpec((flat, cols), lambda t, r: (r, t)),
            pl.BlockSpec((flat, hidden), lambda t, r: (r, t)),
            pl.BlockSpec((flat, hidden), lambda t, r: (r, t)),
        ],
        out_shape=[
            jax.ShapeDtypeStruct((features, 2 * cols), jnp.bfloat16),
            jax.ShapeDtypeStruct((2, features, 2 * cols), jnp.bfloat16),
            jax.ShapeDtypeStruct((features, 2 * cols), jnp.bfloat16),
            jax.ShapeDtypeStruct((features, 2 * hidden), jnp.bfloat16),
            jax.ShapeDtypeStruct((features, 2 * hidden), jnp.bfloat16),
        ],
        compiler_params=pltpu.CompilerParams(vmem_limit_bytes=40 * 1024 * 1024),
        name="unpack_layer",
    )(order, gathered)


def gather_weights(qkv_weight, out_weight, inner_weight, down_weight):
    layers = qkv_weight.shape[0]
    thin = qkv_weight.shape[3]
    cols, hidden = out_weight.shape[1], inner_weight.shape[1]
    piece = jnp.concatenate(
        [qkv_weight.reshape(layers, -1, thin), out_weight, inner_weight, down_weight], axis=1
    )
    width = piece.shape[1]
    piece = piece.reshape(layers, 2, width // 2, thin).transpose(1, 3, 0, 2).reshape(2 * thin, width)
    whole = lax.all_gather(piece, ALL, axis=0, tiled=True)
    features = whole.shape[0] // 4
    return [unpack_layer(whole, layer, thin, features, cols, hidden) for layer in range(layers)]


def split_heads(matrix):
    return matrix.reshape(matrix.shape[0], -1, HEAD).transpose(1, 0, 2)


def join_heads(matrix):
    return matrix.transpose(1, 0, 2).reshape(matrix.shape[1], -1)


def body(
    tokens,
    doc_lengths,
    qkv_weight,
    out_weight,
    inner_weight,
    down_weight,
    query_value_bias,
    hidden_bias,
    shifts,
    gains,
    cotangent,
):
    half_len, features = tokens.shape[1:]
    thin = qkv_weight.shape[3]
    head_cols = qkv_weight.shape[2]
    hidden_cols = inner_weight.shape[1]
    scale_factor = 1.0 / math.sqrt(HEAD)
    tensor_idx = lax.axis_index("tensor")
    dp_idx = lax.axis_index("dp")

    weights = gather_weights(qkv_weight, out_weight, inner_weight, down_weight)
    bias_rows = jnp.concatenate(
        [query_value_bias.reshape(2 * LAYERS, head_cols), hidden_bias.reshape(-1, head_cols)], axis=0
    )
    bias_all = lax.all_gather(bias_rows, "tensor", axis=0, tiled=False)
    qv_bias = bias_all[:, : 2 * LAYERS].reshape(2, LAYERS, 2, head_cols)
    qv_bias = qv_bias.transpose(1, 2, 0, 3).reshape(LAYERS, 2, 2 * head_cols)
    hidden_full = bias_all[:, 2 * LAYERS :].reshape(2, LAYERS, hidden_cols)
    hidden_full = hidden_full.transpose(1, 0, 2).reshape(LAYERS, 2 * hidden_cols)

    position = jnp.arange(half_len, dtype=jnp.int32)
    mine_pos = position + tensor_idx * half_len
    key_pos = jnp.concatenate([mine_pos, position + (1 - tensor_idx) * half_len])
    first_end = doc_lengths[0, 0]
    second_end = first_end + doc_lengths[0, 1]

    def segment(pos):
        return (pos >= first_end).astype(jnp.int32) + (pos >= second_end).astype(jnp.int32)

    same_doc = segment(mine_pos)[:, None] == segment(key_pos)[None, :]

    hidden_state = tokens[0].astype(jnp.float32)
    rounded = tokens[0]
    saved_acts = []
    for layer_idx in range(LAYERS):
        query_w, key_value_w, out_w, inner_w, down_w = weights[layer_idx]
        rows = jnp.concatenate([rounded, swap_halves(rounded)], axis=0)
        query_b = (nn(rounded, query_w) + qv_bias[layer_idx, 0]).astype(jnp.bfloat16)
        key_b = nn(rows, key_value_w[0]).astype(jnp.bfloat16)
        value_b = (nn(rows, key_value_w[1]) + qv_bias[layer_idx, 1]).astype(jnp.bfloat16)
        query_h, key_h, value_h = split_heads(query_b), split_heads(key_b), split_heads(value_b)
        scores = (
            jnp.einsum("hqd,hkd->hqk", query_h, key_h, preferred_element_type=jnp.float32) * scale_factor
        )
        scores = jnp.where(same_doc[None], scores, masked_value)
        row_max = jnp.max(scores, axis=-1, keepdims=True)
        raised = jnp.exp(scores - row_max)
        row_total = jnp.sum(raised, axis=-1, keepdims=True)
        attn_probs = (raised / row_total).astype(jnp.bfloat16)
        log_total = row_max + jnp.log(row_total)
        attended = jnp.einsum("hqk,hkd->hqd", attn_probs, value_h, preferred_element_type=jnp.float32)
        attended_b = join_heads(attended.astype(jnp.bfloat16))
        branch = nt(attended_b, out_w)
        normed, normal_one, inverse_one = layer_norm(
            hidden_state + branch + shifts[layer_idx, 0], gains[layer_idx, 0], shifts[layer_idx, 1]
        )
        normed_low = normed.astype(jnp.bfloat16)
        pre_act = nn(normed_low, inner_w) + hidden_full[layer_idx]
        activated_b = exact_gelu(pre_act).astype(jnp.bfloat16)
        mlp_out = nt(activated_b, down_w)
        hidden_state, normal_two, inverse_two = layer_norm(
            normed + mlp_out + shifts[layer_idx, 2], gains[layer_idx, 1], shifts[layer_idx, 3]
        )
        saved_acts.append(
            (rows, query_h, key_h, value_h, log_total, attended_b, normal_one, inverse_one, normed_low,
             pre_act, activated_b, normal_two, inverse_two)
        )
        rounded = hidden_state.astype(jnp.bfloat16)
    output = hidden_state

    state_grad = cotangent[0]
    weight_parts = [None] * LAYERS
    small_parts = [None] * LAYERS
    for layer_idx in reversed(range(LAYERS)):
        query_w, key_value_w, out_w, inner_w, down_w = weights[layer_idx]
        (rows, query_h, key_h, value_h, log_total, attended_b, normal_one, inverse_one, normed_low,
         pre_act, activated_b, normal_two, inverse_two) = saved_acts[layer_idx]
        pre_two_grad = norm_back(state_grad, normal_two, inverse_two, gains[layer_idx, 1])
        gain_two = jnp.sum(state_grad * normal_two, axis=0)
        beta_two = jnp.sum(state_grad, axis=0)
        shift_two = jnp.sum(pre_two_grad, axis=0)
        mlp_grad_b = pre_two_grad.astype(jnp.bfloat16)
        down_local = tn(mlp_grad_b, activated_b).astype(jnp.bfloat16)
        activated_grad = nn(mlp_grad_b, down_w)
        _, gelu_back = jax.vjp(exact_gelu, pre_act)
        pre_act_grad = gelu_back(activated_grad)[0].astype(jnp.bfloat16)
        hidden_part = jnp.sum(pre_act_grad.astype(jnp.float32), axis=0)
        inner_local = tn(normed_low, pre_act_grad).astype(jnp.bfloat16)
        normed_grad = pre_two_grad + nt(pre_act_grad, inner_w)
        pre_one_grad = norm_back(normed_grad, normal_one, inverse_one, gains[layer_idx, 0])
        gain_one = jnp.sum(normed_grad * normal_one, axis=0)
        beta_one = jnp.sum(normed_grad, axis=0)
        shift_one = jnp.sum(pre_one_grad, axis=0)
        attn_grad_b = pre_one_grad.astype(jnp.bfloat16)
        out_local = tn(attn_grad_b, attended_b).astype(jnp.bfloat16)
        attended_grad = nn(attn_grad_b, out_w).astype(jnp.bfloat16)
        attended_grad_h = split_heads(attended_grad)
        scores = (
            jnp.einsum("hqd,hkd->hqk", query_h, key_h, preferred_element_type=jnp.float32) * scale_factor
        )
        scores = jnp.where(same_doc[None], scores, masked_value)
        probs_full = jnp.exp(scores - log_total)
        probs_low = probs_full.astype(jnp.bfloat16)
        value_grad = jnp.einsum("hqk,hqd->hkd", probs_low, attended_grad_h, preferred_element_type=jnp.float32)
        prob_grad = jnp.einsum("hqd,hkd->hqk", attended_grad_h, value_h, preferred_element_type=jnp.float32)
        row_dot = jnp.sum(prob_grad * probs_full, axis=-1, keepdims=True)
        score_grad = (probs_full * (prob_grad - row_dot)).astype(jnp.bfloat16)
        query_grad = (
            jnp.einsum("hqk,hkd->hqd", score_grad, key_h, preferred_element_type=jnp.float32) * scale_factor
        )
        key_grad = (
            jnp.einsum("hqk,hqd->hkd", score_grad, query_h, preferred_element_type=jnp.float32) * scale_factor
        )
        query_grad_b = join_heads(query_grad.astype(jnp.bfloat16))
        key_grad_b = join_heads(key_grad.astype(jnp.bfloat16))
        value_grad_b = join_heads(value_grad.astype(jnp.bfloat16))
        qv_part = jnp.concatenate(
            [
                jnp.sum(query_grad_b.astype(jnp.float32), axis=0),
                jnp.sum(value_grad_b.astype(jnp.float32), axis=0),
            ]
        )
        query_local = tn(rows[:half_len], query_grad_b).astype(jnp.bfloat16)
        key_local = tn(rows, key_grad_b).astype(jnp.bfloat16)
        value_local = tn(rows, value_grad_b).astype(jnp.bfloat16)
        both = nt(key_grad_b, key_value_w[0]) + nt(value_grad_b, key_value_w[1])
        theirs = swap_halves(both[half_len:].astype(jnp.bfloat16))
        state_grad = (
            pre_one_grad
            + nt(query_grad_b, query_w)
            + both[:half_len]
            + theirs.astype(jnp.float32)
        )
        weight_parts[layer_idx] = (query_local, key_local, value_local, out_local, inner_local, down_local)
        small_parts[layer_idx] = jnp.concatenate(
            [shift_one, beta_one, shift_two, beta_two, gain_one, gain_two, qv_part, hidden_part]
        )
    small = jnp.stack(small_parts).reshape(-1, 2 * hidden_cols).astype(jnp.bfloat16)
    small_rows = small.shape[0]
    small = jnp.pad(small, ((0, -small_rows % 16), (0, 0)))
    with_small = jnp.concatenate([weight_parts[0][5], small], axis=0)
    summed = lax.optimization_barrier(lax.psum((*weight_parts[0][:5], with_small, *weight_parts[1]), ALL))
    small_sum = summed[5][features : features + small_rows].astype(jnp.float32).reshape(LAYERS, -1)
    shift_total = small_sum[:, : 4 * features].reshape(LAYERS, 4, features)
    gain_total = small_sum[:, 4 * features : 6 * features].reshape(LAYERS, 2, features)
    qv_total = lax.dynamic_slice_in_dim(
        small_sum[:, 6 * features : 8 * features].reshape(LAYERS, 2, features), tensor_idx * head_cols, head_cols, 2
    )
    hidden_total = lax.dynamic_slice_in_dim(small_sum[:, 8 * features :], tensor_idx * hidden_cols, hidden_cols, 1)

    def own(layer_idx, which):
        array = summed[6 * layer_idx + which]
        width = array.shape[1] // 2
        part = lax.dynamic_slice(array, (dp_idx * thin, tensor_idx * width), (thin, width))
        return part.astype(jnp.float32).T

    qkv_result = jnp.stack([jnp.stack([own(l, w) for w in range(3)]) for l in range(LAYERS)])
    out_result, inner_result, down_result = (
        jnp.stack([own(l, w) for l in range(LAYERS)]) for w in (3, 4, 5)
    )
    return (
        output[None],
        state_grad[None],
        qkv_result,
        out_result,
        inner_result,
        down_result,
        qv_total,
        hidden_total,
        shift_total,
        gain_total,
    )


def solution(mesh):
    in_specs = (
        P("dp", "tensor", None),
        P("dp", None),
        P(None, None, "tensor", "dp"),
        P(None, "tensor", "dp"),
        P(None, "tensor", "dp"),
        P(None, "tensor", "dp"),
        P(None, None, "tensor"),
        P(None, "tensor"),
        P(),
        P(),
        P("dp", "tensor", None),
    )
    out_specs = (
        P("dp", "tensor", None),
        P("dp", "tensor", None),
        P(None, None, "tensor", "dp"),
        P(None, "tensor", "dp"),
        P(None, "tensor", "dp"),
        P(None, "tensor", "dp"),
        P(None, None, "tensor"),
        P(None, "tensor"),
        P(),
        P(),
    )
    return jax.shard_map(body, mesh=mesh, in_specs=in_specs, out_specs=out_specs, check_vma=False)
```

```python
import math

import jax
import jax.numpy as jnp
from jax import lax
from jax.experimental import pallas as pl
from jax.experimental.pallas import tpu as pltpu
from jax.sharding import PartitionSpec as P

HEAD = 64
LAYERS = 2
ALL = ("tensor", "dp")


epsilon = 1e-06
masked_value = -1e30


def layer_norm(values, gain_vec, shift_vec):
    center = values - jnp.mean(values, axis=-1, keepdims=True)
    variance = jnp.mean(center * center, axis=-1, keepdims=True)
    inverse = lax.rsqrt(variance + epsilon)
    normal = center * inverse
    return normal * gain_vec + shift_vec, normal, inverse


def norm_back(grad, normal, inverse, gain_vec):
    scaled = grad * gain_vec
    mean_one = jnp.mean(scaled, axis=-1, keepdims=True)
    mean_two = jnp.mean(scaled * normal, axis=-1, keepdims=True)
    return inverse * (scaled - mean_one - normal * mean_two)


def exact_gelu(values):
    return jax.nn.gelu(values, approximate=False)


def nn(left, right):
    return lax.dot_general(left, right, (((1,), (0,)), ((), ())), preferred_element_type=jnp.float32)


def nt(left, right):
    return lax.dot_general(left, right, (((1,), (1,)), ((), ())), preferred_element_type=jnp.float32)


def tn(left, right):
    return lax.dot_general(left, right, (((0,), (0,)), ((), ())), preferred_element_type=jnp.float32)


def swap_halves(values):
    return lax.ppermute(values, "tensor", [(0, 1), (1, 0)])


def unpack_kernel(order_ref, packed_ref, query_ref, key_value_ref, out_ref, inner_ref, down_ref):
    picked = jnp.dot(order_ref[...], packed_ref[...], preferred_element_type=jnp.float32)
    picked = picked.astype(jnp.bfloat16)
    rows, cols = query_ref.shape
    hidden = inner_ref.shape[1] // 2
    query_ref[...] = picked[:rows, :cols]
    key_value_ref[0] = picked[:rows, cols : 2 * cols]
    key_value_ref[1] = picked[:rows, 2 * cols : 3 * cols]
    out_ref[...] = picked[:rows, 3 * cols : 4 * cols]
    inner_ref[:, :hidden] = picked[:rows, 4 * cols :]
    inner_ref[:, hidden:] = picked[rows:, :hidden]
    down_ref[...] = picked[rows:, hidden:]


def unpack_layer(gathered, layer_idx, thin, features, cols, hidden):
    group = 8
    tall = 2 * thin * group
    flat = thin * group
    width = gathered.shape[1] // LAYERS
    blocks = features // flat
    spot = jnp.arange(tall, dtype=jnp.int32)
    half = spot // flat
    source = (spot % flat) // thin * (2 * thin) + half * thin + spot % thin
    order = (source[:, None] == jnp.arange(tall, dtype=jnp.int32)[None, :]).astype(jnp.bfloat16)
    return pl.pallas_call(
        unpack_kernel,
        grid=(2, blocks),
        in_specs=[
            pl.BlockSpec((tall, tall), lambda t, r: (0, 0)),
            pl.BlockSpec((tall, width), lambda t, r: (t * blocks + r, layer_idx)),
        ],
        out_specs=[
            pl.BlockSpec((flat, cols), lambda t, r: (r, t)),
            pl.BlockSpec((2, flat, cols), lambda t, r: (0, r, t)),
            pl.BlockSpec((flat, cols), lambda t, r: (r, t)),
            pl.BlockSpec((flat, hidden), lambda t, r: (r, t)),
            pl.BlockSpec((flat, hidden), lambda t, r: (r, t)),
        ],
        out_shape=[
            jax.ShapeDtypeStruct((features, 2 * cols), jnp.bfloat16),
            jax.ShapeDtypeStruct((2, features, 2 * cols), jnp.bfloat16),
            jax.ShapeDtypeStruct((features, 2 * cols), jnp.bfloat16),
            jax.ShapeDtypeStruct((features, 2 * hidden), jnp.bfloat16),
            jax.ShapeDtypeStruct((features, 2 * hidden), jnp.bfloat16),
        ],
        compiler_params=pltpu.CompilerParams(vmem_limit_bytes=40 * 1024 * 1024),
        name="unpack_layer",
    )(order, gathered)


def gather_weights(qkv_weight, out_weight, inner_weight, down_weight):
    layers = qkv_weight.shape[0]
    thin = qkv_weight.shape[3]
    cols, hidden = out_weight.shape[1], inner_weight.shape[1]
    piece = jnp.concatenate(
        [qkv_weight.reshape(layers, -1, thin), out_weight, inner_weight, down_weight], axis=1
    )
    width = piece.shape[1]
    piece = piece.reshape(layers, 2, width // 2, thin).transpose(1, 3, 0, 2).reshape(2 * thin, width)
    whole = lax.all_gather(piece, ALL, axis=0, tiled=True)
    features = whole.shape[0] // 4
    return [unpack_layer(whole, layer, thin, features, cols, hidden) for layer in range(layers)]


def coords(flat):
    dp = flat >> 1
    return [(flat & 1) * 2 + (dp >> 5), (dp >> 3) & 3, (dp >> 1) & 3, dp & 1]


def flat_index(x, z, y, core):
    return ((((x & 1) * 4 + z) * 4 + y) * 2 + core) * 2 + (x >> 1)


def partner(pos, kind):
    return pos ^ 1 if kind == 0 else (pos ^ 1) ^ 2


def exchange(values, axis, kind=0):
    pairs = []
    for flat in range(128):
        place = coords(flat)
        place[axis] = place[axis] ^ 1 if axis == 3 else partner(place[axis], kind)
        pairs.append((flat, flat_index(*place)))
    return lax.ppermute(values, ("dp", "tensor"), pairs)


def add_low(left, right):
    return (left.astype(jnp.float32) + right.astype(jnp.float32)).astype(jnp.bfloat16)


def pick(values, index, dim):
    return lax.dynamic_slice_in_dim(values, index, 1, dim)


def halve_axis(values, place, axis, dim, kind):
    me = place[axis]
    first, second = partner(me, kind), partner(me, 1 - kind)
    sent = jnp.concatenate(
        [pick(values, first, dim), pick(values, partner(first, 1 - kind), dim)], axis=dim
    )
    got = exchange(sent, axis, kind)
    kept = jnp.concatenate([pick(values, me, dim), pick(values, second, dim)], axis=dim)
    kept = add_low(kept, got)
    last = exchange(lax.slice_in_dim(kept, 1, 2, axis=dim), axis, 1 - kind)
    return add_low(lax.slice_in_dim(kept, 0, 1, axis=dim), last)


def scatter_group(values, place, order):
    cols = values.shape[-1]
    values = values.reshape(4, 4, 4, -1, cols)
    half = cols // 2
    axis = order[0]
    parts = [halve_axis(values[..., k * half : (k + 1) * half], place, axis, axis, k) for k in range(2)]
    values = jnp.concatenate(parts, axis=-1)
    for axis in order[1:]:
        values = halve_axis(values, place, axis, axis, 0)
    return values.reshape(-1, cols)


def sum_all(values):
    values = values + exchange(values, 3)
    for axis in range(3):
        values = values + exchange(values, axis, 0)
        values = values + exchange(values, axis, 1)
    return values


def column_parts(matrix, offset, width):
    step = matrix.shape[1] // 2
    return [lax.dynamic_slice_in_dim(matrix, t * step + offset, width, 1) for t in range(2)]


def grads_of(left, right, offset, width):
    return [tn(left, part).astype(jnp.bfloat16) for part in column_parts(right, offset, width)]


def reduce_core(make, core, place, order):
    sent = make(1 - core)
    got = exchange(sent, 3)
    return scatter_group(add_low(make(core), got), place, order)


def split_heads(matrix):
    return matrix.reshape(matrix.shape[0], -1, HEAD).transpose(1, 0, 2)


def join_heads(matrix):
    return matrix.transpose(1, 0, 2).reshape(matrix.shape[1], -1)


def body(
    tokens,
    doc_lengths,
    qkv_weight,
    out_weight,
    inner_weight,
    down_weight,
    query_value_bias,
    hidden_bias,
    shifts,
    gains,
    cotangent,
):
    half_len, features = tokens.shape[1:]
    thin = qkv_weight.shape[3]
    head_cols = qkv_weight.shape[2]
    hidden_cols = inner_weight.shape[1]
    scale_factor = 1.0 / math.sqrt(HEAD)
    tensor_idx = lax.axis_index("tensor")
    dp_idx = lax.axis_index("dp")
    core = dp_idx & 1
    place = [tensor_idx * 2 + (dp_idx >> 5), (dp_idx >> 3) & 3, (dp_idx >> 1) & 3]

    weights = gather_weights(qkv_weight, out_weight, inner_weight, down_weight)
    bias_rows = jnp.concatenate(
        [query_value_bias.reshape(2 * LAYERS, head_cols), hidden_bias.reshape(-1, head_cols)], axis=0
    )
    bias_all = lax.all_gather(bias_rows, "tensor", axis=0, tiled=False)
    qv_bias = bias_all[:, : 2 * LAYERS].reshape(2, LAYERS, 2, head_cols)
    qv_bias = qv_bias.transpose(1, 2, 0, 3).reshape(LAYERS, 2, 2 * head_cols)
    hidden_full = bias_all[:, 2 * LAYERS :].reshape(2, LAYERS, hidden_cols)
    hidden_full = hidden_full.transpose(1, 0, 2).reshape(LAYERS, 2 * hidden_cols)

    position = jnp.arange(half_len, dtype=jnp.int32)
    mine_pos = position + tensor_idx * half_len
    key_pos = jnp.concatenate([mine_pos, position + (1 - tensor_idx) * half_len])
    first_end = doc_lengths[0, 0]
    second_end = first_end + doc_lengths[0, 1]

    def segment(pos):
        return (pos >= first_end).astype(jnp.int32) + (pos >= second_end).astype(jnp.int32)

    same_doc = segment(mine_pos)[:, None] == segment(key_pos)[None, :]

    hidden_state = tokens[0].astype(jnp.float32)
    rounded = tokens[0]
    saved_acts = []
    for layer_idx in range(LAYERS):
        query_w, key_value_w, out_w, inner_w, down_w = weights[layer_idx]
        rows = jnp.concatenate([rounded, swap_halves(rounded)], axis=0)
        query_b = (nn(rounded, query_w) + qv_bias[layer_idx, 0]).astype(jnp.bfloat16)
        key_b = nn(rows, key_value_w[0]).astype(jnp.bfloat16)
        value_b = (nn(rows, key_value_w[1]) + qv_bias[layer_idx, 1]).astype(jnp.bfloat16)
        query_h, key_h, value_h = split_heads(query_b), split_heads(key_b), split_heads(value_b)
        scores = (
            jnp.einsum("hqd,hkd->hqk", query_h, key_h, preferred_element_type=jnp.float32) * scale_factor
        )
        scores = jnp.where(same_doc[None], scores, masked_value)
        row_max = jnp.max(scores, axis=-1, keepdims=True)
        raised = jnp.exp(scores - row_max)
        row_total = jnp.sum(raised, axis=-1, keepdims=True)
        attn_probs = (raised / row_total).astype(jnp.bfloat16)
        log_total = row_max + jnp.log(row_total)
        attended = jnp.einsum("hqk,hkd->hqd", attn_probs, value_h, preferred_element_type=jnp.float32)
        attended_b = join_heads(attended.astype(jnp.bfloat16))
        branch = nt(attended_b, out_w)
        normed, normal_one, inverse_one = layer_norm(
            hidden_state + branch + shifts[layer_idx, 0], gains[layer_idx, 0], shifts[layer_idx, 1]
        )
        normed_low = normed.astype(jnp.bfloat16)
        pre_act = nn(normed_low, inner_w) + hidden_full[layer_idx]
        activated_b = exact_gelu(pre_act).astype(jnp.bfloat16)
        mlp_out = nt(activated_b, down_w)
        hidden_state, normal_two, inverse_two = layer_norm(
            normed + mlp_out + shifts[layer_idx, 2], gains[layer_idx, 1], shifts[layer_idx, 3]
        )
        saved_acts.append(
            (rows, query_h, key_h, value_h, log_total, attended_b, normal_one, inverse_one, normed_low,
             pre_act, activated_b, normal_two, inverse_two)
        )
        rounded = hidden_state.astype(jnp.bfloat16)
    output = hidden_state

    state_grad = cotangent[0]
    weight_parts = [None] * LAYERS
    small_parts = [None] * LAYERS
    for layer_idx in reversed(range(LAYERS)):
        query_w, key_value_w, out_w, inner_w, down_w = weights[layer_idx]
        (rows, query_h, key_h, value_h, log_total, attended_b, normal_one, inverse_one, normed_low,
         pre_act, activated_b, normal_two, inverse_two) = saved_acts[layer_idx]
        pre_two_grad = norm_back(state_grad, normal_two, inverse_two, gains[layer_idx, 1])
        gain_two = jnp.sum(state_grad * normal_two, axis=0)
        beta_two = jnp.sum(state_grad, axis=0)
        shift_two = jnp.sum(pre_two_grad, axis=0)
        mlp_grad_b = pre_two_grad.astype(jnp.bfloat16)
        half_hidden = hidden_cols // 2
        if layer_idx > 0:
            down_local = tn(mlp_grad_b, activated_b).astype(jnp.bfloat16)
        else:
            down_own = reduce_core(
                lambda side: jnp.stack(grads_of(mlp_grad_b, activated_b, side * half_hidden, half_hidden)),
                core, place, (2, 0, 1),
            )
        activated_grad = nn(mlp_grad_b, down_w)
        _, gelu_back = jax.vjp(exact_gelu, pre_act)
        pre_act_grad = gelu_back(activated_grad)[0].astype(jnp.bfloat16)
        hidden_part = jnp.sum(pre_act_grad.astype(jnp.float32), axis=0)
        if layer_idx > 0:
            inner_local = tn(normed_low, pre_act_grad).astype(jnp.bfloat16)
        else:
            inner_own = reduce_core(
                lambda side: jnp.stack(grads_of(normed_low, pre_act_grad, side * half_hidden, half_hidden)),
                core, place, (1, 2, 0),
            )
        normed_grad = pre_two_grad + nt(pre_act_grad, inner_w)
        pre_one_grad = norm_back(normed_grad, normal_one, inverse_one, gains[layer_idx, 0])
        gain_one = jnp.sum(normed_grad * normal_one, axis=0)
        beta_one = jnp.sum(normed_grad, axis=0)
        shift_one = jnp.sum(pre_one_grad, axis=0)
        attn_grad_b = pre_one_grad.astype(jnp.bfloat16)
        if layer_idx > 0:
            out_local = tn(attn_grad_b, attended_b).astype(jnp.bfloat16)
        attended_grad = nn(attn_grad_b, out_w).astype(jnp.bfloat16)
        attended_grad_h = split_heads(attended_grad)
        scores = (
            jnp.einsum("hqd,hkd->hqk", query_h, key_h, preferred_element_type=jnp.float32) * scale_factor
        )
        scores = jnp.where(same_doc[None], scores, masked_value)
        probs_full = jnp.exp(scores - log_total)
        probs_low = probs_full.astype(jnp.bfloat16)
        value_grad = jnp.einsum("hqk,hqd->hkd", probs_low, attended_grad_h, preferred_element_type=jnp.float32)
        prob_grad = jnp.einsum("hqd,hkd->hqk", attended_grad_h, value_h, preferred_element_type=jnp.float32)
        row_dot = jnp.sum(prob_grad * probs_full, axis=-1, keepdims=True)
        score_grad = (probs_full * (prob_grad - row_dot)).astype(jnp.bfloat16)
        query_grad = (
            jnp.einsum("hqk,hkd->hqd", score_grad, key_h, preferred_element_type=jnp.float32) * scale_factor
        )
        key_grad = (
            jnp.einsum("hqk,hqd->hkd", score_grad, query_h, preferred_element_type=jnp.float32) * scale_factor
        )
        query_grad_b = join_heads(query_grad.astype(jnp.bfloat16))
        key_grad_b = join_heads(key_grad.astype(jnp.bfloat16))
        value_grad_b = join_heads(value_grad.astype(jnp.bfloat16))
        qv_part = jnp.concatenate(
            [
                jnp.sum(query_grad_b.astype(jnp.float32), axis=0),
                jnp.sum(value_grad_b.astype(jnp.float32), axis=0),
            ]
        )
        if layer_idx > 0:
            query_local = tn(rows[:half_len], query_grad_b).astype(jnp.bfloat16)
            key_local = tn(rows, key_grad_b).astype(jnp.bfloat16)
            value_local = tn(rows, value_grad_b).astype(jnp.bfloat16)
            weight_parts[layer_idx] = lax.optimization_barrier(
                lax.psum((query_local, key_local, value_local, out_local, inner_local, down_local), ALL)
            )
        else:
            padding = ((0, half_len), (0, 0))
            query_pad, attn_pad, attended_pad = (
                jnp.pad(v, padding) for v in (query_grad_b, attn_grad_b, attended_b)
            )

            def attn_grads(side):
                left = jnp.where(side == 0, rows, attn_pad)
                one = grads_of(rows, jnp.where(side == 0, query_pad, value_grad_b), 0, head_cols)
                two = grads_of(left, jnp.where(side == 0, key_grad_b, attended_pad), 0, head_cols)
                return jnp.stack([jnp.concatenate(pair, axis=1) for pair in zip(one, two)])

            attn_own = reduce_core(attn_grads, core, place, (0, 1, 2))
        both = nt(key_grad_b, key_value_w[0]) + nt(value_grad_b, key_value_w[1])
        theirs = swap_halves(both[half_len:].astype(jnp.bfloat16))
        state_grad = (
            pre_one_grad
            + nt(query_grad_b, query_w)
            + both[:half_len]
            + theirs.astype(jnp.float32)
        )
        small_parts[layer_idx] = jnp.concatenate(
            [shift_one, beta_one, shift_two, beta_two, gain_one, gain_two, qv_part, hidden_part]
        )
    small_sum = sum_all(jnp.stack(small_parts).reshape(-1, features)).reshape(LAYERS, -1)
    shift_total = small_sum[:, : 4 * features].reshape(LAYERS, 4, features)
    gain_total = small_sum[:, 4 * features : 6 * features].reshape(LAYERS, 2, features)
    qv_total = lax.dynamic_slice_in_dim(
        small_sum[:, 6 * features : 8 * features].reshape(LAYERS, 2, features), tensor_idx * head_cols, head_cols, 2
    )
    hidden_total = lax.dynamic_slice_in_dim(small_sum[:, 8 * features :], tensor_idx * hidden_cols, hidden_cols, 1)

    first_rows = jnp.concatenate([attn_own, inner_own, down_own], axis=1)
    theirs = exchange(lax.dynamic_slice_in_dim(first_rows, (1 - core) * thin, thin, 0), 3)
    mine = lax.dynamic_slice_in_dim(first_rows, core * thin, thin, 0)
    low_side = jnp.where(core == 0, mine, theirs).reshape(thin, 3, -1)
    high_side = jnp.where(core == 0, theirs, mine).reshape(thin, 3, -1)
    first_own = jnp.concatenate([low_side, high_side], axis=2).reshape(thin, -1)

    def own(which):
        array = weight_parts[1][which]
        width = array.shape[1] // 2
        return lax.dynamic_slice(array, (dp_idx * thin, tensor_idx * width), (thin, width))

    second_own = jnp.concatenate([own(which) for which in range(6)], axis=1)
    both_own = jnp.stack([first_own, second_own]).astype(jnp.float32)

    def result(start, stop):
        return both_own[:, :, start:stop].transpose(0, 2, 1)

    qkv_result = result(0, 3 * head_cols).reshape(LAYERS, 3, head_cols, thin)
    out_result = result(3 * head_cols, 4 * head_cols)
    inner_result = result(4 * head_cols, 4 * head_cols + hidden_cols)
    down_result = result(4 * head_cols + hidden_cols, 4 * head_cols + 2 * hidden_cols)
    return (
        output[None],
        state_grad[None],
        qkv_result,
        out_result,
        inner_result,
        down_result,
        qv_total,
        hidden_total,
        shift_total,
        gain_total,
    )


def solution(mesh):
    in_specs = (
        P("dp", "tensor", None),
        P("dp", None),
        P(None, None, "tensor", "dp"),
        P(None, "tensor", "dp"),
        P(None, "tensor", "dp"),
        P(None, "tensor", "dp"),
        P(None, None, "tensor"),
        P(None, "tensor"),
        P(),
        P(),
        P("dp", "tensor", None),
    )
    out_specs = (
        P("dp", "tensor", None),
        P("dp", "tensor", None),
        P(None, None, "tensor", "dp"),
        P(None, "tensor", "dp"),
        P(None, "tensor", "dp"),
        P(None, "tensor", "dp"),
        P(None, None, "tensor"),
        P(None, "tensor"),
        P(),
        P(),
    )
    return jax.shard_map(body, mesh=mesh, in_specs=in_specs, out_specs=out_specs, check_vma=False)
```

```python
import math

import jax
import jax.numpy as jnp
from jax import lax
from jax.experimental import pallas as pl
from jax.experimental.pallas import tpu as pltpu
from jax.sharding import PartitionSpec as P

HEAD = 64
LAYERS = 2
ALL = ("tensor", "dp")


epsilon = 1e-06
masked_value = -1e30


def layer_norm(values, gain_vec, shift_vec):
    center = values - jnp.mean(values, axis=-1, keepdims=True)
    variance = jnp.mean(center * center, axis=-1, keepdims=True)
    inverse = lax.rsqrt(variance + epsilon)
    normal = center * inverse
    return normal * gain_vec + shift_vec, normal, inverse


def norm_back(grad, normal, inverse, gain_vec):
    scaled = grad * gain_vec
    mean_one = jnp.mean(scaled, axis=-1, keepdims=True)
    mean_two = jnp.mean(scaled * normal, axis=-1, keepdims=True)
    return inverse * (scaled - mean_one - normal * mean_two)


def exact_gelu(values):
    return jax.nn.gelu(values, approximate=False)


def nn(left, right):
    return lax.dot_general(left, right, (((1,), (0,)), ((), ())), preferred_element_type=jnp.float32)


def nt(left, right):
    return lax.dot_general(left, right, (((1,), (1,)), ((), ())), preferred_element_type=jnp.float32)


def tn(left, right):
    return lax.dot_general(left, right, (((0,), (0,)), ((), ())), preferred_element_type=jnp.float32)


def swap_halves(values):
    return lax.ppermute(values, "tensor", [(0, 1), (1, 0)])


def unpack_kernel(order_ref, packed_ref, query_ref, key_value_ref, out_ref, inner_ref, down_ref):
    picked = jnp.dot(order_ref[...], packed_ref[...], preferred_element_type=jnp.float32)
    picked = picked.astype(jnp.bfloat16)
    rows, cols = query_ref.shape
    hidden = inner_ref.shape[1] // 2
    query_ref[...] = picked[:rows, :cols]
    key_value_ref[0] = picked[:rows, cols : 2 * cols]
    key_value_ref[1] = picked[:rows, 2 * cols : 3 * cols]
    out_ref[...] = picked[:rows, 3 * cols : 4 * cols]
    inner_ref[:, :hidden] = picked[:rows, 4 * cols :]
    inner_ref[:, hidden:] = picked[rows:, :hidden]
    down_ref[...] = picked[rows:, hidden:]


def unpack_layer(gathered, layer_idx, thin, features, cols, hidden):
    group = 8
    tall = 2 * thin * group
    flat = thin * group
    width = gathered.shape[1] // LAYERS
    blocks = features // flat
    spot = jnp.arange(tall, dtype=jnp.int32)
    half = spot // flat
    source = (spot % flat) // thin * (2 * thin) + half * thin + spot % thin
    order = (source[:, None] == jnp.arange(tall, dtype=jnp.int32)[None, :]).astype(jnp.bfloat16)
    return pl.pallas_call(
        unpack_kernel,
        grid=(2, blocks),
        in_specs=[
            pl.BlockSpec((tall, tall), lambda t, r: (0, 0)),
            pl.BlockSpec((tall, width), lambda t, r: (t * blocks + r, layer_idx)),
        ],
        out_specs=[
            pl.BlockSpec((flat, cols), lambda t, r: (r, t)),
            pl.BlockSpec((2, flat, cols), lambda t, r: (0, r, t)),
            pl.BlockSpec((flat, cols), lambda t, r: (r, t)),
            pl.BlockSpec((flat, hidden), lambda t, r: (r, t)),
            pl.BlockSpec((flat, hidden), lambda t, r: (r, t)),
        ],
        out_shape=[
            jax.ShapeDtypeStruct((features, 2 * cols), jnp.bfloat16),
            jax.ShapeDtypeStruct((2, features, 2 * cols), jnp.bfloat16),
            jax.ShapeDtypeStruct((features, 2 * cols), jnp.bfloat16),
            jax.ShapeDtypeStruct((features, 2 * hidden), jnp.bfloat16),
            jax.ShapeDtypeStruct((features, 2 * hidden), jnp.bfloat16),
        ],
        compiler_params=pltpu.CompilerParams(vmem_limit_bytes=40 * 1024 * 1024),
        name="unpack_layer",
    )(order, gathered)


def gather_weights(qkv_weight, out_weight, inner_weight, down_weight):
    layers = qkv_weight.shape[0]
    thin = qkv_weight.shape[3]
    cols, hidden = out_weight.shape[1], inner_weight.shape[1]
    piece = jnp.concatenate(
        [qkv_weight.reshape(layers, -1, thin), out_weight, inner_weight, down_weight], axis=1
    )
    width = piece.shape[1]
    piece = piece.reshape(layers, 2, width // 2, thin).transpose(1, 3, 0, 2).reshape(2 * thin, width)
    whole = lax.all_gather(piece, ALL, axis=0, tiled=True)
    features = whole.shape[0] // 4
    return [unpack_layer(whole, layer, thin, features, cols, hidden) for layer in range(layers)]


def coords(flat):
    dp = flat >> 1
    return [(flat & 1) * 2 + (dp >> 5), (dp >> 3) & 3, (dp >> 1) & 3, dp & 1]


def flat_index(x, z, y, core):
    return ((((x & 1) * 4 + z) * 4 + y) * 2 + core) * 2 + (x >> 1)


def partner(pos, kind):
    return pos ^ 1 if kind == 0 else (pos ^ 1) ^ 2


def exchange(values, axis, kind=0):
    pairs = []
    for flat in range(128):
        place = coords(flat)
        place[axis] = place[axis] ^ 1 if axis == 3 else partner(place[axis], kind)
        pairs.append((flat, flat_index(*place)))
    return lax.ppermute(values, ("dp", "tensor"), pairs)


def add_low(left, right):
    return (left.astype(jnp.float32) + right.astype(jnp.float32)).astype(jnp.bfloat16)


def pick(values, index, dim):
    return lax.dynamic_slice_in_dim(values, index, 1, dim)


def halve_first(values, place, axis, kind):
    me = place[axis]
    first, second = partner(me, kind), partner(me, 1 - kind)
    sent = jnp.concatenate(
        [pick(values, first, axis), pick(values, partner(first, 1 - kind), axis)], axis=axis
    )
    got = exchange(sent, axis, kind)
    kept = jnp.concatenate([pick(values, me, axis), pick(values, second, axis)], axis=axis)
    return add_low(kept, got)


def halve_second(kept, axis, kind):
    last = exchange(lax.slice_in_dim(kept, 1, 2, axis=axis), axis, 1 - kind)
    return add_low(lax.slice_in_dim(kept, 0, 1, axis=axis), last)


def scatter_rounds(values, place, order):
    cols = values.shape[-1]
    values = values.reshape(4, 4, 4, -1, cols)
    parts = [values[..., : cols // 2], values[..., cols // 2 :]]
    for step, axis in enumerate(order):
        if step == 1:
            parts = [jnp.concatenate(parts, axis=-1)]
        parts = yield [halve_first(part, place, axis, kind) for kind, part in enumerate(parts)]
        parts = yield [halve_second(part, axis, kind) for kind, part in enumerate(parts)]


def sum_rounds(values):
    values = yield values + exchange(values, 3)
    for axis in range(3):
        for kind in range(2):
            values = yield values + exchange(values, axis, kind)


def pack_kernel(*refs):
    packed = refs[-1]
    row = 0
    for ref in refs[:-1]:
        for part in range(ref.shape[1] // packed.shape[1]):
            packed[row : row + 1, :] = ref[:, part * packed.shape[1] : (part + 1) * packed.shape[1]]
            row += 1


def pack_rows(vectors, features):
    rows = sum(vector.shape[0] for vector in vectors) // features
    return pl.pallas_call(
        pack_kernel,
        out_shape=jax.ShapeDtypeStruct((rows, features), jnp.float32),
        name="pack_rows",
    )(*[vector.reshape(1, -1) for vector in vectors])


def column_parts(matrix, offset, width):
    step = matrix.shape[1] // 2
    return [lax.dynamic_slice_in_dim(matrix, t * step + offset, width, 1) for t in range(2)]


def grads_of(left, right, offset, width):
    return [tn(left, part).astype(jnp.bfloat16) for part in column_parts(right, offset, width)]


def reduce_core(make, core):
    got = exchange(make(1 - core), 3)
    return add_low(make(core), got)


def split_heads(matrix):
    return matrix.reshape(matrix.shape[0], -1, HEAD).transpose(1, 0, 2)


def join_heads(matrix):
    return matrix.transpose(1, 0, 2).reshape(matrix.shape[1], -1)


def body(
    tokens,
    doc_lengths,
    qkv_weight,
    out_weight,
    inner_weight,
    down_weight,
    query_value_bias,
    hidden_bias,
    shifts,
    gains,
    cotangent,
):
    half_len, features = tokens.shape[1:]
    thin = qkv_weight.shape[3]
    head_cols = qkv_weight.shape[2]
    hidden_cols = inner_weight.shape[1]
    scale_factor = 1.0 / math.sqrt(HEAD)
    tensor_idx = lax.axis_index("tensor")
    dp_idx = lax.axis_index("dp")
    core = dp_idx & 1
    place = [tensor_idx * 2 + (dp_idx >> 5), (dp_idx >> 3) & 3, (dp_idx >> 1) & 3]

    weights = gather_weights(qkv_weight, out_weight, inner_weight, down_weight)
    bias_rows = jnp.concatenate(
        [query_value_bias.reshape(2 * LAYERS, head_cols), hidden_bias.reshape(-1, head_cols)], axis=0
    )
    bias_all = lax.all_gather(bias_rows, "tensor", axis=0, tiled=False)
    qv_bias = bias_all[:, : 2 * LAYERS].reshape(2, LAYERS, 2, head_cols)
    qv_bias = qv_bias.transpose(1, 2, 0, 3).reshape(LAYERS, 2, 2 * head_cols)
    hidden_full = bias_all[:, 2 * LAYERS :].reshape(2, LAYERS, hidden_cols)
    hidden_full = hidden_full.transpose(1, 0, 2).reshape(LAYERS, 2 * hidden_cols)

    position = jnp.arange(half_len, dtype=jnp.int32)
    mine_pos = position + tensor_idx * half_len
    key_pos = jnp.concatenate([mine_pos, position + (1 - tensor_idx) * half_len])
    first_end = doc_lengths[0, 0]
    second_end = first_end + doc_lengths[0, 1]

    def segment(pos):
        return (pos >= first_end).astype(jnp.int32) + (pos >= second_end).astype(jnp.int32)

    same_doc = segment(mine_pos)[:, None] == segment(key_pos)[None, :]

    hidden_state = tokens[0].astype(jnp.float32)
    rounded = tokens[0]
    saved_acts = []
    for layer_idx in range(LAYERS):
        query_w, key_value_w, out_w, inner_w, down_w = weights[layer_idx]
        rows = jnp.concatenate([rounded, swap_halves(rounded)], axis=0)
        query_b = (nn(rounded, query_w) + qv_bias[layer_idx, 0]).astype(jnp.bfloat16)
        key_b = nn(rows, key_value_w[0]).astype(jnp.bfloat16)
        value_b = (nn(rows, key_value_w[1]) + qv_bias[layer_idx, 1]).astype(jnp.bfloat16)
        query_h, key_h, value_h = split_heads(query_b), split_heads(key_b), split_heads(value_b)
        scores = (
            jnp.einsum("hqd,hkd->hqk", query_h, key_h, preferred_element_type=jnp.float32) * scale_factor
        )
        scores = jnp.where(same_doc[None], scores, masked_value)
        row_max = jnp.max(scores, axis=-1, keepdims=True)
        raised = jnp.exp(scores - row_max)
        row_total = jnp.sum(raised, axis=-1, keepdims=True)
        attn_probs = (raised / row_total).astype(jnp.bfloat16)
        log_total = row_max + jnp.log(row_total)
        attended = jnp.einsum("hqk,hkd->hqd", attn_probs, value_h, preferred_element_type=jnp.float32)
        attended_b = join_heads(attended.astype(jnp.bfloat16))
        branch = nt(attended_b, out_w)
        normed, normal_one, inverse_one = layer_norm(
            hidden_state + branch + shifts[layer_idx, 0], gains[layer_idx, 0], shifts[layer_idx, 1]
        )
        normed_low = normed.astype(jnp.bfloat16)
        pre_act = nn(normed_low, inner_w) + hidden_full[layer_idx]
        activated_b = exact_gelu(pre_act).astype(jnp.bfloat16)
        mlp_out = nt(activated_b, down_w)
        hidden_state, normal_two, inverse_two = layer_norm(
            normed + mlp_out + shifts[layer_idx, 2], gains[layer_idx, 1], shifts[layer_idx, 3]
        )
        saved_acts.append(
            (rows, query_h, key_h, value_h, log_total, attended_b, normal_one, inverse_one, normed_low,
             pre_act, activated_b, normal_two, inverse_two)
        )
        rounded = hidden_state.astype(jnp.bfloat16)
    output = hidden_state

    state_grad = cotangent[0]
    weight_parts = [None] * LAYERS
    small_parts = [None] * LAYERS
    for layer_idx in reversed(range(LAYERS)):
        query_w, key_value_w, out_w, inner_w, down_w = weights[layer_idx]
        (rows, query_h, key_h, value_h, log_total, attended_b, normal_one, inverse_one, normed_low,
         pre_act, activated_b, normal_two, inverse_two) = saved_acts[layer_idx]
        pre_two_grad = norm_back(state_grad, normal_two, inverse_two, gains[layer_idx, 1])
        gain_two = jnp.sum(state_grad * normal_two, axis=0)
        beta_two = jnp.sum(state_grad, axis=0)
        shift_two = jnp.sum(pre_two_grad, axis=0)
        mlp_grad_b = pre_two_grad.astype(jnp.bfloat16)
        half_hidden = hidden_cols // 2
        if layer_idx > 0:
            down_local = tn(mlp_grad_b, activated_b).astype(jnp.bfloat16)
        else:
            down_part = reduce_core(
                lambda side: jnp.stack(grads_of(mlp_grad_b, activated_b, side * half_hidden, half_hidden)), core
            )
        activated_grad = nn(mlp_grad_b, down_w)
        _, gelu_back = jax.vjp(exact_gelu, pre_act)
        pre_act_grad = gelu_back(activated_grad)[0].astype(jnp.bfloat16)
        hidden_part = jnp.sum(pre_act_grad.astype(jnp.float32), axis=0)
        if layer_idx > 0:
            inner_local = tn(normed_low, pre_act_grad).astype(jnp.bfloat16)
        else:
            inner_part = reduce_core(
                lambda side: jnp.stack(grads_of(normed_low, pre_act_grad, side * half_hidden, half_hidden)), core
            )
            wide = scatter_rounds(jnp.concatenate([inner_part, down_part], axis=-1), place, (1, 2, 0))
            wide_parts = next(wide)
        normed_grad = pre_two_grad + nt(pre_act_grad, inner_w)
        pre_one_grad = norm_back(normed_grad, normal_one, inverse_one, gains[layer_idx, 0])
        gain_one = jnp.sum(normed_grad * normal_one, axis=0)
        beta_one = jnp.sum(normed_grad, axis=0)
        shift_one = jnp.sum(pre_one_grad, axis=0)
        attn_grad_b = pre_one_grad.astype(jnp.bfloat16)
        if layer_idx > 0:
            out_local = tn(attn_grad_b, attended_b).astype(jnp.bfloat16)
        attended_grad = nn(attn_grad_b, out_w).astype(jnp.bfloat16)
        attended_grad_h = split_heads(attended_grad)
        scores = (
            jnp.einsum("hqd,hkd->hqk", query_h, key_h, preferred_element_type=jnp.float32) * scale_factor
        )
        scores = jnp.where(same_doc[None], scores, masked_value)
        probs_full = jnp.exp(scores - log_total)
        probs_low = probs_full.astype(jnp.bfloat16)
        value_grad = jnp.einsum("hqk,hqd->hkd", probs_low, attended_grad_h, preferred_element_type=jnp.float32)
        prob_grad = jnp.einsum("hqd,hkd->hqk", attended_grad_h, value_h, preferred_element_type=jnp.float32)
        row_dot = jnp.sum(prob_grad * probs_full, axis=-1, keepdims=True)
        score_grad = (probs_full * (prob_grad - row_dot)).astype(jnp.bfloat16)
        query_grad = (
            jnp.einsum("hqk,hkd->hqd", score_grad, key_h, preferred_element_type=jnp.float32) * scale_factor
        )
        key_grad = (
            jnp.einsum("hqk,hqd->hkd", score_grad, query_h, preferred_element_type=jnp.float32) * scale_factor
        )
        if layer_idx == 0:
            wide_parts, query_grad, key_grad, value_grad = lax.optimization_barrier(
                (wide_parts, query_grad, key_grad, value_grad)
            )
            wide_parts = wide.send(wide_parts)
        query_grad_b = join_heads(query_grad.astype(jnp.bfloat16))
        key_grad_b = join_heads(key_grad.astype(jnp.bfloat16))
        value_grad_b = join_heads(value_grad.astype(jnp.bfloat16))
        qv_part = [
            jnp.sum(query_grad_b.astype(jnp.float32), axis=0),
            jnp.sum(value_grad_b.astype(jnp.float32), axis=0),
        ]
        if layer_idx > 0:
            query_local = tn(rows[:half_len], query_grad_b).astype(jnp.bfloat16)
            key_local = tn(rows, key_grad_b).astype(jnp.bfloat16)
            value_local = tn(rows, value_grad_b).astype(jnp.bfloat16)
            weight_parts[layer_idx] = lax.optimization_barrier(
                lax.psum((query_local, key_local, value_local, out_local, inner_local, down_local), ALL)
            )
        else:
            padding = ((0, half_len), (0, 0))
            query_pad, attn_pad, attended_pad = (
                jnp.pad(v, padding) for v in (query_grad_b, attn_grad_b, attended_b)
            )

            def attn_grads(side):
                left = jnp.where(side == 0, rows, attn_pad)
                one = grads_of(rows, jnp.where(side == 0, query_pad, value_grad_b), 0, head_cols)
                two = grads_of(left, jnp.where(side == 0, key_grad_b, attended_pad), 0, head_cols)
                return jnp.stack([jnp.concatenate(pair, axis=1) for pair in zip(one, two)])

            attn_part = reduce_core(attn_grads, core)
        both = nt(key_grad_b, key_value_w[0]) + nt(value_grad_b, key_value_w[1])
        theirs = swap_halves(both[half_len:].astype(jnp.bfloat16))
        state_grad = (
            pre_one_grad
            + nt(query_grad_b, query_w)
            + both[:half_len]
            + theirs.astype(jnp.float32)
        )
        small_parts[layer_idx] = [
            shift_one, beta_one, shift_two, beta_two, gain_one, gain_two, *qv_part, hidden_part
        ]
    small = pack_rows(small_parts[0] + small_parts[1], features)
    wide_parts, attn_part, small = lax.optimization_barrier((wide_parts, attn_part, small))
    attn = scatter_rounds(attn_part, place, (0, 1, 2))
    tiny = sum_rounds(small)
    wide_parts, attn_parts, small = lax.optimization_barrier((wide.send(wide_parts), next(attn), next(tiny)))
    for _ in range(3):
        wide_parts, attn_parts, small = lax.optimization_barrier(
            (wide.send(wide_parts), attn.send(attn_parts), tiny.send(small))
        )
    for _ in range(2):
        attn_parts, small = lax.optimization_barrier((attn.send(attn_parts), tiny.send(small)))
    small_sum = tiny.send(small).reshape(LAYERS, -1)
    shift_total = small_sum[:, : 4 * features].reshape(LAYERS, 4, features)
    gain_total = small_sum[:, 4 * features : 6 * features].reshape(LAYERS, 2, features)
    qv_total = lax.dynamic_slice_in_dim(
        small_sum[:, 6 * features : 8 * features].reshape(LAYERS, 2, features), tensor_idx * head_cols, head_cols, 2
    )
    hidden_total = lax.dynamic_slice_in_dim(small_sum[:, 8 * features :], tensor_idx * hidden_cols, hidden_cols, 1)

    first_rows = jnp.concatenate(
        [attn_parts[0].reshape(2 * thin, -1), wide_parts[0].reshape(2 * thin, -1)], axis=1
    )
    theirs = exchange(lax.dynamic_slice_in_dim(first_rows, (1 - core) * thin, thin, 0), 3)
    mine = lax.dynamic_slice_in_dim(first_rows, core * thin, thin, 0)
    low_side = jnp.where(core == 0, mine, theirs).reshape(thin, 3, -1)
    high_side = jnp.where(core == 0, theirs, mine).reshape(thin, 3, -1)
    first_own = jnp.concatenate([low_side, high_side], axis=2).reshape(thin, -1)

    def own(which):
        array = weight_parts[1][which]
        width = array.shape[1] // 2
        return lax.dynamic_slice(array, (dp_idx * thin, tensor_idx * width), (thin, width))

    second_own = jnp.concatenate([own(which) for which in range(6)], axis=1)
    both_own = jnp.stack([first_own, second_own]).astype(jnp.float32)

    def result(start, stop):
        return both_own[:, :, start:stop].transpose(0, 2, 1)

    qkv_result = result(0, 3 * head_cols).reshape(LAYERS, 3, head_cols, thin)
    out_result = result(3 * head_cols, 4 * head_cols)
    inner_result = result(4 * head_cols, 4 * head_cols + hidden_cols)
    down_result = result(4 * head_cols + hidden_cols, 4 * head_cols + 2 * hidden_cols)
    return (
        output[None],
        state_grad[None],
        qkv_result,
        out_result,
        inner_result,
        down_result,
        qv_total,
        hidden_total,
        shift_total,
        gain_total,
    )


def solution(mesh):
    in_specs = (
        P("dp", "tensor", None),
        P("dp", None),
        P(None, None, "tensor", "dp"),
        P(None, "tensor", "dp"),
        P(None, "tensor", "dp"),
        P(None, "tensor", "dp"),
        P(None, None, "tensor"),
        P(None, "tensor"),
        P(),
        P(),
        P("dp", "tensor", None),
    )
    out_specs = (
        P("dp", "tensor", None),
        P("dp", "tensor", None),
        P(None, None, "tensor", "dp"),
        P(None, "tensor", "dp"),
        P(None, "tensor", "dp"),
        P(None, "tensor", "dp"),
        P(None, None, "tensor"),
        P(None, "tensor"),
        P(),
        P(),
    )
    return jax.shard_map(body, mesh=mesh, in_specs=in_specs, out_specs=out_specs, check_vma=False)
```

```python
import functools
import math

import jax
import jax.numpy as jnp
from jax import lax
from jax.experimental import pallas as pl
from jax.experimental.layout import Layout, with_layout_constraint
from jax.experimental.pallas import tpu as pltpu
from jax.sharding import PartitionSpec as P

HEAD = 64
LAYERS = 2
ALL = ("tensor", "dp")


epsilon = 1e-06
masked_value = -1e30


def layer_norm(values, gain_vec, shift_vec):
    center = values - jnp.mean(values, axis=-1, keepdims=True)
    variance = jnp.mean(center * center, axis=-1, keepdims=True)
    inverse = lax.rsqrt(variance + epsilon)
    normal = center * inverse
    return normal * gain_vec + shift_vec, normal, inverse


def norm_back(grad, normal, inverse, gain_vec):
    scaled = grad * gain_vec
    mean_one = jnp.mean(scaled, axis=-1, keepdims=True)
    mean_two = jnp.mean(scaled * normal, axis=-1, keepdims=True)
    return inverse * (scaled - mean_one - normal * mean_two)


def exact_gelu(values):
    return jax.nn.gelu(values, approximate=False)


def nn(left, right):
    return lax.dot_general(left, right, (((1,), (0,)), ((), ())), preferred_element_type=jnp.float32)


def nt(left, right):
    return lax.dot_general(left, right, (((1,), (1,)), ((), ())), preferred_element_type=jnp.float32)


def tn(left, right):
    return lax.dot_general(left, right, (((0,), (0,)), ((), ())), preferred_element_type=jnp.float32)


def swap_halves(values):
    return lax.ppermute(values, "tensor", [(0, 1), (1, 0)])


def unpack_kernel(order_ref, packed_ref, query_ref, key_value_ref, out_ref, inner_ref, down_ref):
    picked = jnp.dot(order_ref[...], packed_ref[...], preferred_element_type=jnp.float32)
    picked = picked.astype(jnp.bfloat16)
    rows, cols = query_ref.shape
    hidden = inner_ref.shape[1] // 2
    query_ref[...] = picked[:rows, :cols]
    key_value_ref[0] = picked[:rows, cols : 2 * cols]
    key_value_ref[1] = picked[:rows, 2 * cols : 3 * cols]
    out_ref[...] = picked[:rows, 3 * cols : 4 * cols]
    inner_ref[:, :hidden] = picked[:rows, 4 * cols :]
    inner_ref[:, hidden:] = picked[rows:, :hidden]
    down_ref[...] = picked[rows:, hidden:]


def unpack_layer(gathered, layer_idx, thin, features, cols, hidden):
    group = 8
    tall = 2 * thin * group
    flat = thin * group
    width = gathered.shape[1] // LAYERS
    blocks = features // flat
    spot = jnp.arange(tall, dtype=jnp.int32)
    half = spot // flat
    source = (spot % flat) // thin * (2 * thin) + half * thin + spot % thin
    order = (source[:, None] == jnp.arange(tall, dtype=jnp.int32)[None, :]).astype(jnp.bfloat16)
    return pl.pallas_call(
        unpack_kernel,
        grid=(2, blocks),
        in_specs=[
            pl.BlockSpec((tall, tall), lambda t, r: (0, 0)),
            pl.BlockSpec((tall, width), lambda t, r: (t * blocks + r, layer_idx)),
        ],
        out_specs=[
            pl.BlockSpec((flat, cols), lambda t, r: (r, t)),
            pl.BlockSpec((2, flat, cols), lambda t, r: (0, r, t)),
            pl.BlockSpec((flat, cols), lambda t, r: (r, t)),
            pl.BlockSpec((flat, hidden), lambda t, r: (r, t)),
            pl.BlockSpec((flat, hidden), lambda t, r: (r, t)),
        ],
        out_shape=[
            jax.ShapeDtypeStruct((features, 2 * cols), jnp.bfloat16),
            jax.ShapeDtypeStruct((2, features, 2 * cols), jnp.bfloat16),
            jax.ShapeDtypeStruct((features, 2 * cols), jnp.bfloat16),
            jax.ShapeDtypeStruct((features, 2 * hidden), jnp.bfloat16),
            jax.ShapeDtypeStruct((features, 2 * hidden), jnp.bfloat16),
        ],
        compiler_params=pltpu.CompilerParams(vmem_limit_bytes=40 * 1024 * 1024),
        name="unpack_layer",
    )(order, gathered)


def gather_weights(qkv_weight, out_weight, inner_weight, down_weight):
    layers = qkv_weight.shape[0]
    thin = qkv_weight.shape[3]
    cols, hidden = out_weight.shape[1], inner_weight.shape[1]
    piece = jnp.concatenate(
        [qkv_weight.reshape(layers, -1, thin), out_weight, inner_weight, down_weight], axis=1
    )
    width = piece.shape[1]
    piece = piece.reshape(layers, 2, width // 2, thin).transpose(1, 3, 0, 2).reshape(2 * thin, width)
    whole = lax.all_gather(piece, ALL, axis=0, tiled=True)
    features = whole.shape[0] // 4
    return [unpack_layer(whole, layer, thin, features, cols, hidden) for layer in range(layers)]


def coords(flat):
    dp = flat >> 1
    return [(flat & 1) * 2 + (dp >> 5), (dp >> 3) & 3, (dp >> 1) & 3, dp & 1]


def flat_index(x, z, y, core):
    return ((((x & 1) * 4 + z) * 4 + y) * 2 + core) * 2 + (x >> 1)


def partner(pos, kind):
    return pos ^ 1 if kind == 0 else (pos ^ 1) ^ 2


def exchange(values, axis, kind=0):
    pairs = []
    for flat in range(128):
        place = coords(flat)
        place[axis] = place[axis] ^ 1 if axis == 3 else partner(place[axis], kind)
        pairs.append((flat, flat_index(*place)))
    return lax.ppermute(values, ("dp", "tensor"), pairs)


def add_low(left, right):
    return (left.astype(jnp.float32) + right.astype(jnp.float32)).astype(jnp.bfloat16)


def pick(values, index, dim):
    return lax.dynamic_slice_in_dim(values, index, 1, dim)


def halve_first(values, place, axis, kind):
    me = place[axis]
    first, second = partner(me, kind), partner(me, 1 - kind)
    sent = jnp.concatenate(
        [pick(values, first, axis), pick(values, partner(first, 1 - kind), axis)], axis=axis
    )
    got = exchange(sent, axis, kind)
    kept = jnp.concatenate([pick(values, me, axis), pick(values, second, axis)], axis=axis)
    return add_low(kept, got)


def halve_second(kept, axis, kind):
    last = exchange(lax.slice_in_dim(kept, 1, 2, axis=axis), axis, 1 - kind)
    return add_low(lax.slice_in_dim(kept, 0, 1, axis=axis), last)


def scatter_rounds(parts, place, order):
    parts = [part.reshape(4, 4, 4, -1, part.shape[-1]) for part in parts]
    for step, axis in enumerate(order):
        if step == 1:
            parts = [jnp.concatenate(parts, axis=-1)]
        parts = yield [halve_first(part, place, axis, kind) for kind, part in enumerate(parts)]
        parts = yield [halve_second(part, axis, kind) for kind, part in enumerate(parts)]


def sum_rounds(values):
    values = yield values + exchange(values, 3)
    for axis in range(3):
        for kind in range(2):
            values = yield values + exchange(values, axis, kind)


def pack_kernel(*refs):
    packed = refs[-1]
    row = 0
    for ref in refs[:-1]:
        for part in range(ref.shape[1] // packed.shape[1]):
            packed[row : row + 1, :] = ref[:, part * packed.shape[1] : (part + 1) * packed.shape[1]]
            row += 1


def pack_rows(vectors, features):
    rows = sum(vector.shape[1] for vector in vectors) // features
    return pl.pallas_call(
        pack_kernel,
        out_shape=jax.ShapeDtypeStruct((rows, features), jnp.float32),
        name="pack_rows",
    )(*vectors)


def row_major(matrix):
    return with_layout_constraint(matrix, Layout(major_to_minor=(0, 1)))


def column_parts(matrix, offset, width):
    step = matrix.shape[1] // 2
    return [lax.dynamic_slice_in_dim(matrix, t * step + offset, width, 1) for t in range(2)]


def grads_of(left, right, offset, width):
    return jnp.stack([row_major(tn(left, part).astype(jnp.bfloat16)) for part in column_parts(right, offset, width)])


def reduce_core(make, core):
    got = exchange(make(1 - core), 3)
    return add_low(make(core), got)


WINDOW = 32


def cut_kernel(thin, cuts, place_ref, first_ref, *refs):
    summed, outs, (window, copied) = refs[:6], refs[6:10], refs[10:]
    start = pl.multiple_of(place_ref[0], 16)
    copies = []
    for index, array in enumerate(summed):
        width = cuts[index + 1] - cuts[index]
        first_col = pl.multiple_of(place_ref[2] * width, 128)
        copies.append(
            pltpu.make_async_copy(
                array.at[pl.ds(start, WINDOW), pl.ds(first_col, width)],
                window.at[:, pl.ds(cuts[index], width)],
                copied.at[index],
            )
        )
        copies[-1].start()
    for copy in copies:
        copy.wait()
    spot = jax.lax.broadcasted_iota(jnp.int32, (WINDOW, 128), 0)
    lane = jax.lax.broadcasted_iota(jnp.int32, (WINDOW, 128), 1)
    contract = (((0,), (0,)), ((), ()))
    for layer_idx, (source, offset) in enumerate(((first_ref, 0), (window, place_ref[1]))):
        chosen = jnp.where((spot == lane + offset) & (lane < thin), 1.0, 0.0)[: source.shape[0]]
        for out, low, high in zip(outs, (0, cuts[3], cuts[4], cuts[5]), (cuts[3], cuts[4], cuts[5], cuts[6])):
            step = 384
            for col in range(low, high, step):
                part = source[:, col : col + step].astype(jnp.float32)
                turned = lax.dot_general(part, chosen, contract, preferred_element_type=jnp.float32)
                out[layer_idx, col - low : col - low + step, :] = turned[:, :thin]


def cut_rows(first_own, summed, dp_idx, tensor_idx, thin, head_cols, hidden_cols):
    features = summed[0].shape[0]
    start = jnp.minimum(dp_idx * thin // 16 * 16, features - WINDOW)
    place = jnp.stack([start, dp_idx * thin - start, tensor_idx]).astype(jnp.int32)
    cuts = [0]
    for array in summed:
        cuts.append(cuts[-1] + array.shape[1] // 2)
    widths = (3 * head_cols, head_cols, hidden_cols, hidden_cols)
    vmem = pl.BlockSpec(memory_space=pltpu.VMEM)
    return pl.pallas_call(
        functools.partial(cut_kernel, thin, tuple(cuts)),
        in_specs=[pl.BlockSpec(memory_space=pltpu.SMEM), vmem] + [pl.BlockSpec(memory_space=pl.ANY)] * 6,
        out_specs=[vmem] * 4,
        out_shape=[jax.ShapeDtypeStruct((LAYERS, width, thin), jnp.float32) for width in widths],
        scratch_shapes=[pltpu.VMEM((WINDOW, cuts[-1]), jnp.bfloat16), pltpu.SemaphoreType.DMA((6,))],
        compiler_params=pltpu.CompilerParams(vmem_limit_bytes=32 * 1024 * 1024),
        name="cut_rows",
    )(place, jnp.pad(first_own, ((0, 16 - thin), (0, 0))), *summed)


def split_heads(matrix):
    return matrix.reshape(matrix.shape[0], -1, HEAD).transpose(1, 0, 2)


def join_heads(matrix):
    return matrix.transpose(1, 0, 2).reshape(matrix.shape[1], -1)


def body(
    tokens,
    doc_lengths,
    qkv_weight,
    out_weight,
    inner_weight,
    down_weight,
    query_value_bias,
    hidden_bias,
    shifts,
    gains,
    cotangent,
):
    half_len, features = tokens.shape[1:]
    thin = qkv_weight.shape[3]
    head_cols = qkv_weight.shape[2]
    hidden_cols = inner_weight.shape[1]
    scale_factor = 1.0 / math.sqrt(HEAD)
    tensor_idx = lax.axis_index("tensor")
    dp_idx = lax.axis_index("dp")
    core = dp_idx & 1
    place = [tensor_idx * 2 + (dp_idx >> 5), (dp_idx >> 3) & 3, (dp_idx >> 1) & 3]

    weights = gather_weights(qkv_weight, out_weight, inner_weight, down_weight)
    bias_rows = jnp.concatenate(
        [query_value_bias.reshape(2 * LAYERS, head_cols), hidden_bias.reshape(-1, head_cols)], axis=0
    )
    bias_all = lax.all_gather(bias_rows, "tensor", axis=0, tiled=False)
    qv_bias = bias_all[:, : 2 * LAYERS].reshape(2, LAYERS, 2, head_cols)
    qv_bias = qv_bias.transpose(1, 2, 0, 3).reshape(LAYERS, 2, 2 * head_cols)
    hidden_full = bias_all[:, 2 * LAYERS :].reshape(2, LAYERS, hidden_cols)
    hidden_full = hidden_full.transpose(1, 0, 2).reshape(LAYERS, 2 * hidden_cols)

    position = jnp.arange(half_len, dtype=jnp.int32)
    mine_pos = position + tensor_idx * half_len
    key_pos = jnp.concatenate([mine_pos, position + (1 - tensor_idx) * half_len])
    first_end = doc_lengths[0, 0]
    second_end = first_end + doc_lengths[0, 1]

    def segment(pos):
        return (pos >= first_end).astype(jnp.int32) + (pos >= second_end).astype(jnp.int32)

    same_doc = segment(mine_pos)[:, None] == segment(key_pos)[None, :]

    hidden_state = tokens[0].astype(jnp.float32)
    rounded = tokens[0]
    saved_acts = []
    for layer_idx in range(LAYERS):
        query_w, key_value_w, out_w, inner_w, down_w = weights[layer_idx]
        rows = jnp.concatenate([rounded, swap_halves(rounded)], axis=0)
        query_b = (nn(rounded, query_w) + qv_bias[layer_idx, 0]).astype(jnp.bfloat16)
        key_b = nn(rows, key_value_w[0]).astype(jnp.bfloat16)
        value_b = (nn(rows, key_value_w[1]) + qv_bias[layer_idx, 1]).astype(jnp.bfloat16)
        query_h, key_h, value_h = split_heads(query_b), split_heads(key_b), split_heads(value_b)
        scores = (
            jnp.einsum("hqd,hkd->hqk", query_h, key_h, preferred_element_type=jnp.float32) * scale_factor
        )
        scores = jnp.where(same_doc[None], scores, masked_value)
        row_max = jnp.max(scores, axis=-1, keepdims=True)
        raised = jnp.exp(scores - row_max)
        row_total = jnp.sum(raised, axis=-1, keepdims=True)
        attn_probs = (raised / row_total).astype(jnp.bfloat16)
        log_total = row_max + jnp.log(row_total)
        attended = jnp.einsum("hqk,hkd->hqd", attn_probs, value_h, preferred_element_type=jnp.float32)
        attended_b = join_heads(attended.astype(jnp.bfloat16))
        branch = nt(attended_b, out_w)
        normed, normal_one, inverse_one = layer_norm(
            hidden_state + branch + shifts[layer_idx, 0], gains[layer_idx, 0], shifts[layer_idx, 1]
        )
        normed_low = normed.astype(jnp.bfloat16)
        pre_act = nn(normed_low, inner_w) + hidden_full[layer_idx]
        activated_b = exact_gelu(pre_act).astype(jnp.bfloat16)
        mlp_out = nt(activated_b, down_w)
        hidden_state, normal_two, inverse_two = layer_norm(
            normed + mlp_out + shifts[layer_idx, 2], gains[layer_idx, 1], shifts[layer_idx, 3]
        )
        saved_acts.append(
            (rows, query_h, key_h, value_h, log_total, attended_b, normal_one, inverse_one, normed_low,
             pre_act, activated_b, normal_two, inverse_two)
        )
        rounded = hidden_state.astype(jnp.bfloat16)
    output = hidden_state

    state_grad = cotangent[0]
    weight_parts = [None] * LAYERS
    small_parts = [None] * LAYERS
    for layer_idx in reversed(range(LAYERS)):
        query_w, key_value_w, out_w, inner_w, down_w = weights[layer_idx]
        (rows, query_h, key_h, value_h, log_total, attended_b, normal_one, inverse_one, normed_low,
         pre_act, activated_b, normal_two, inverse_two) = saved_acts[layer_idx]
        pre_two_grad = norm_back(state_grad, normal_two, inverse_two, gains[layer_idx, 1])
        gain_two = jnp.sum(state_grad * normal_two, axis=0, keepdims=True)
        beta_two = jnp.sum(state_grad, axis=0, keepdims=True)
        shift_two = jnp.sum(pre_two_grad, axis=0, keepdims=True)
        mlp_grad_b = pre_two_grad.astype(jnp.bfloat16)
        half_hidden = hidden_cols // 2
        if layer_idx > 0:
            down_local = tn(mlp_grad_b, activated_b).astype(jnp.bfloat16)
        else:
            down_part = reduce_core(
                lambda side: grads_of(mlp_grad_b, activated_b, side * half_hidden, half_hidden), core
            )
        activated_grad = nn(mlp_grad_b, down_w)
        _, gelu_back = jax.vjp(exact_gelu, pre_act)
        pre_act_grad = gelu_back(activated_grad)[0].astype(jnp.bfloat16)
        hidden_part = jnp.sum(pre_act_grad.astype(jnp.float32), axis=0, keepdims=True)
        if layer_idx > 0:
            inner_local = tn(normed_low, pre_act_grad).astype(jnp.bfloat16)
        else:
            inner_part = reduce_core(
                lambda side: grads_of(normed_low, pre_act_grad, side * half_hidden, half_hidden), core
            )
            wide = scatter_rounds([inner_part, down_part], place, (1, 2, 0))
            wide_parts = next(wide)
        normed_grad = pre_two_grad + nt(pre_act_grad, inner_w)
        pre_one_grad = norm_back(normed_grad, normal_one, inverse_one, gains[layer_idx, 0])
        gain_one = jnp.sum(normed_grad * normal_one, axis=0, keepdims=True)
        beta_one = jnp.sum(normed_grad, axis=0, keepdims=True)
        shift_one = jnp.sum(pre_one_grad, axis=0, keepdims=True)
        attn_grad_b = pre_one_grad.astype(jnp.bfloat16)
        if layer_idx > 0:
            out_local = tn(attn_grad_b, attended_b).astype(jnp.bfloat16)
        attended_grad = nn(attn_grad_b, out_w).astype(jnp.bfloat16)
        attended_grad_h = split_heads(attended_grad)
        scores = (
            jnp.einsum("hqd,hkd->hqk", query_h, key_h, preferred_element_type=jnp.float32) * scale_factor
        )
        scores = jnp.where(same_doc[None], scores, masked_value)
        probs_full = jnp.exp(scores - log_total)
        probs_low = probs_full.astype(jnp.bfloat16)
        value_grad = jnp.einsum("hqk,hqd->hkd", probs_low, attended_grad_h, preferred_element_type=jnp.float32)
        prob_grad = jnp.einsum("hqd,hkd->hqk", attended_grad_h, value_h, preferred_element_type=jnp.float32)
        row_dot = jnp.sum(prob_grad * probs_full, axis=-1, keepdims=True)
        score_grad = (probs_full * (prob_grad - row_dot)).astype(jnp.bfloat16)
        query_grad = (
            jnp.einsum("hqk,hkd->hqd", score_grad, key_h, preferred_element_type=jnp.float32) * scale_factor
        )
        key_grad = (
            jnp.einsum("hqk,hqd->hkd", score_grad, query_h, preferred_element_type=jnp.float32) * scale_factor
        )
        query_grad_b = join_heads(query_grad.astype(jnp.bfloat16))
        key_grad_b = join_heads(key_grad.astype(jnp.bfloat16))
        value_grad_b = join_heads(value_grad.astype(jnp.bfloat16))
        qv_part = [
            jnp.sum(query_grad_b.astype(jnp.float32), axis=0, keepdims=True),
            jnp.sum(value_grad_b.astype(jnp.float32), axis=0, keepdims=True),
        ]
        if layer_idx > 0:
            query_local = tn(rows[:half_len], query_grad_b).astype(jnp.bfloat16)
            key_local = tn(rows, key_grad_b).astype(jnp.bfloat16)
            value_local = tn(rows, value_grad_b).astype(jnp.bfloat16)
            locals_all = (query_local, key_local, value_local, out_local, inner_local, down_local)
            weight_parts[layer_idx] = lax.psum(tuple(row_major(part) for part in locals_all), ALL)
        else:
            padding = ((0, half_len), (0, 0))
            query_pad, attn_pad, attended_pad = (
                jnp.pad(v, padding) for v in (query_grad_b, attn_grad_b, attended_b)
            )

            def first_grads(side):
                return grads_of(rows, jnp.where(side == 0, query_pad, value_grad_b), 0, head_cols)

            def second_grads(side):
                left = jnp.where(side == 0, rows, attn_pad)
                return grads_of(left, jnp.where(side == 0, key_grad_b, attended_pad), 0, head_cols)

            attn_parts = [reduce_core(first_grads, core), reduce_core(second_grads, core)]
        both = nt(key_grad_b, key_value_w[0]) + nt(value_grad_b, key_value_w[1])
        theirs = swap_halves(both[half_len:].astype(jnp.bfloat16))
        state_grad = (
            pre_one_grad
            + nt(query_grad_b, query_w)
            + both[:half_len]
            + theirs.astype(jnp.float32)
        )
        small_parts[layer_idx] = [
            shift_one, beta_one, shift_two, beta_two, gain_one, gain_two, *qv_part, hidden_part
        ]
    small = pack_rows(small_parts[0] + small_parts[1], features)
    wide_parts, attn_parts, small = lax.optimization_barrier((wide_parts, attn_parts, small))
    attn = scatter_rounds(attn_parts, place, (0, 1, 2))
    tiny = sum_rounds(small)
    wide_parts, attn_parts, small = lax.optimization_barrier(
        (wide.send(wide_parts), next(attn), next(tiny))
    )
    for _ in range(4):
        wide_parts, attn_parts, small = lax.optimization_barrier(
            (wide.send(wide_parts), attn.send(attn_parts), tiny.send(small))
        )
    attn_parts, small = lax.optimization_barrier((attn.send(attn_parts), tiny.send(small)))
    small_sum = tiny.send(small).reshape(LAYERS, -1)
    first_rows = jnp.concatenate(
        [attn_parts[0].reshape(2 * thin, -1), wide_parts[0].reshape(2 * thin, -1)], axis=1
    )
    theirs = exchange(lax.dynamic_slice_in_dim(first_rows, (1 - core) * thin, thin, 0), 3)
    mine = lax.dynamic_slice_in_dim(first_rows, core * thin, thin, 0)
    low_side = jnp.where(core == 0, mine, theirs).reshape(thin, 3, -1)
    high_side = jnp.where(core == 0, theirs, mine).reshape(thin, 3, -1)
    first_own = jnp.concatenate([low_side, high_side], axis=2).reshape(thin, -1)
    first_own, small_sum, summed = lax.optimization_barrier((first_own, small_sum, weight_parts[1]))
    qkv_result, out_result, inner_result, down_result = cut_rows(
        first_own, summed, dp_idx, tensor_idx, thin, head_cols, hidden_cols
    )
    qkv_result = qkv_result.reshape(LAYERS, 3, head_cols, thin)
    shift_total = small_sum[:, : 4 * features].reshape(LAYERS, 4, features)
    gain_total = small_sum[:, 4 * features : 6 * features].reshape(LAYERS, 2, features)
    qv_total = lax.dynamic_slice_in_dim(
        small_sum[:, 6 * features : 8 * features].reshape(LAYERS, 2, features), tensor_idx * head_cols, head_cols, 2
    )
    hidden_total = lax.dynamic_slice_in_dim(small_sum[:, 8 * features :], tensor_idx * hidden_cols, hidden_cols, 1)
    return (
        output[None],
        state_grad[None],
        qkv_result,
        out_result,
        inner_result,
        down_result,
        qv_total,
        hidden_total,
        shift_total,
        gain_total,
    )


def solution(mesh):
    in_specs = (
        P("dp", "tensor", None),
        P("dp", None),
        P(None, None, "tensor", "dp"),
        P(None, "tensor", "dp"),
        P(None, "tensor", "dp"),
        P(None, "tensor", "dp"),
        P(None, None, "tensor"),
        P(None, "tensor"),
        P(),
        P(),
        P("dp", "tensor", None),
    )
    out_specs = (
        P("dp", "tensor", None),
        P("dp", "tensor", None),
        P(None, None, "tensor", "dp"),
        P(None, "tensor", "dp"),
        P(None, "tensor", "dp"),
        P(None, "tensor", "dp"),
        P(None, None, "tensor"),
        P(None, "tensor"),
        P(),
        P(),
    )
    return jax.shard_map(body, mesh=mesh, in_specs=in_specs, out_specs=out_specs, check_vma=False)
```

```python
import functools
import math

import jax
import jax.numpy as jnp
from jax import lax
from jax.experimental import pallas as pl
from jax.experimental.layout import Layout, with_layout_constraint
from jax.experimental.pallas import tpu as pltpu
from jax.sharding import PartitionSpec as P

HEAD = 64
LAYERS = 2
ALL = ("tensor", "dp")


epsilon = 1e-06
masked_value = -1e30


def layer_norm(values, gain_vec, shift_vec):
    center = values - jnp.mean(values, axis=-1, keepdims=True)
    variance = jnp.mean(center * center, axis=-1, keepdims=True)
    inverse = lax.rsqrt(variance + epsilon)
    normal = center * inverse
    return normal * gain_vec + shift_vec, normal, inverse


def norm_back(grad, normal, inverse, gain_vec):
    scaled = grad * gain_vec
    mean_one = jnp.mean(scaled, axis=-1, keepdims=True)
    mean_two = jnp.mean(scaled * normal, axis=-1, keepdims=True)
    return inverse * (scaled - mean_one - normal * mean_two)


def exact_gelu(values):
    return jax.nn.gelu(values, approximate=False)


def nn(left, right):
    return lax.dot_general(left, right, (((1,), (0,)), ((), ())), preferred_element_type=jnp.float32)


def nt(left, right):
    return lax.dot_general(left, right, (((1,), (1,)), ((), ())), preferred_element_type=jnp.float32)


def tn(left, right):
    return lax.dot_general(left, right, (((0,), (0,)), ((), ())), preferred_element_type=jnp.float32)


def swap_halves(values):
    return lax.ppermute(values, "tensor", [(0, 1), (1, 0)])


def unpack_kernel(order_ref, packed_ref, query_ref, key_value_ref, out_ref, inner_ref, down_ref):
    picked = jnp.dot(order_ref[...], packed_ref[...], preferred_element_type=jnp.float32)
    picked = picked.astype(jnp.bfloat16)
    rows, cols = query_ref.shape
    hidden = inner_ref.shape[1] // 2
    query_ref[...] = picked[:rows, :cols]
    key_value_ref[0] = picked[:rows, cols : 2 * cols]
    key_value_ref[1] = picked[:rows, 2 * cols : 3 * cols]
    out_ref[...] = picked[:rows, 3 * cols : 4 * cols]
    inner_ref[:, :hidden] = picked[:rows, 4 * cols :]
    inner_ref[:, hidden:] = picked[rows:, :hidden]
    down_ref[...] = picked[rows:, hidden:]


def unpack_layer(gathered, layer_idx, thin, features, cols, hidden):
    group = 8
    tall = 2 * thin * group
    flat = thin * group
    width = gathered.shape[1] // LAYERS
    blocks = features // flat
    spot = jnp.arange(tall, dtype=jnp.int32)
    half = spot // flat
    source = (spot % flat) // thin * (2 * thin) + half * thin + spot % thin
    order = (source[:, None] == jnp.arange(tall, dtype=jnp.int32)[None, :]).astype(jnp.bfloat16)
    return pl.pallas_call(
        unpack_kernel,
        grid=(2, blocks),
        in_specs=[
            pl.BlockSpec((tall, tall), lambda t, r: (0, 0)),
            pl.BlockSpec((tall, width), lambda t, r: (t * blocks + r, layer_idx)),
        ],
        out_specs=[
            pl.BlockSpec((flat, cols), lambda t, r: (r, t)),
            pl.BlockSpec((2, flat, cols), lambda t, r: (0, r, t)),
            pl.BlockSpec((flat, cols), lambda t, r: (r, t)),
            pl.BlockSpec((flat, hidden), lambda t, r: (r, t)),
            pl.BlockSpec((flat, hidden), lambda t, r: (r, t)),
        ],
        out_shape=[
            jax.ShapeDtypeStruct((features, 2 * cols), jnp.bfloat16),
            jax.ShapeDtypeStruct((2, features, 2 * cols), jnp.bfloat16),
            jax.ShapeDtypeStruct((features, 2 * cols), jnp.bfloat16),
            jax.ShapeDtypeStruct((features, 2 * hidden), jnp.bfloat16),
            jax.ShapeDtypeStruct((features, 2 * hidden), jnp.bfloat16),
        ],
        compiler_params=pltpu.CompilerParams(vmem_limit_bytes=40 * 1024 * 1024),
        name="unpack_layer",
    )(order, gathered)


def gather_weights(qkv_weight, out_weight, inner_weight, down_weight):
    layers = qkv_weight.shape[0]
    thin = qkv_weight.shape[3]
    cols, hidden = out_weight.shape[1], inner_weight.shape[1]
    piece = jnp.concatenate(
        [qkv_weight.reshape(layers, -1, thin), out_weight, inner_weight, down_weight], axis=1
    )
    width = piece.shape[1]
    piece = piece.reshape(layers, 2, width // 2, thin).transpose(1, 3, 0, 2).reshape(2 * thin, width)
    whole = lax.all_gather(piece, ALL, axis=0, tiled=True)
    features = whole.shape[0] // 4
    return [unpack_layer(whole, layer, thin, features, cols, hidden) for layer in range(layers)]


def coords(flat):
    dp = flat >> 1
    return [(flat & 1) * 2 + (dp >> 5), (dp >> 3) & 3, (dp >> 1) & 3, dp & 1]


def flat_index(x, z, y, core):
    return ((((x & 1) * 4 + z) * 4 + y) * 2 + core) * 2 + (x >> 1)


def partner(pos, kind):
    return pos ^ 1 if kind == 0 else (pos ^ 1) ^ 2


def exchange(values, axis, kind=0):
    pairs = []
    for flat in range(128):
        place = coords(flat)
        place[axis] = place[axis] ^ 1 if axis == 3 else partner(place[axis], kind)
        pairs.append((flat, flat_index(*place)))
    return lax.ppermute(values, ("dp", "tensor"), pairs)


def add_low(left, right):
    return (left.astype(jnp.float32) + right.astype(jnp.float32)).astype(jnp.bfloat16)


def pick(values, index, dim):
    return lax.dynamic_slice_in_dim(values, index, 1, dim)


def halve_first(values, place, axis, kind):
    me = place[axis]
    first, second = partner(me, kind), partner(me, 1 - kind)
    sent = jnp.concatenate(
        [pick(values, first, axis), pick(values, partner(first, 1 - kind), axis)], axis=axis
    )
    got = exchange(sent, axis, kind)
    kept = jnp.concatenate([pick(values, me, axis), pick(values, second, axis)], axis=axis)
    return add_low(kept, got)


def halve_second(kept, axis, kind):
    last = exchange(lax.slice_in_dim(kept, 1, 2, axis=axis), axis, 1 - kind)
    return add_low(lax.slice_in_dim(kept, 0, 1, axis=axis), last)


def scatter_rounds(parts, place, order):
    parts = [part.reshape(4, 4, 4, -1, part.shape[-1]) for part in parts]
    for step, axis in enumerate(order):
        if step == 1:
            parts = [jnp.concatenate(parts, axis=-1)]
        parts = yield [halve_first(part, place, axis, kind) for kind, part in enumerate(parts)]
        parts = yield [halve_second(part, axis, kind) for kind, part in enumerate(parts)]


def sum_rounds(values):
    values = yield values + exchange(values, 3)
    for axis in range(3):
        for kind in range(2):
            values = yield values + exchange(values, axis, kind)


def pack_kernel(*refs):
    packed = refs[-1]
    row = 0
    for ref in refs[:-1]:
        for part in range(ref.shape[1] // packed.shape[1]):
            packed[row : row + 1, :] = ref[:, part * packed.shape[1] : (part + 1) * packed.shape[1]]
            row += 1


def pack_rows(vectors, features):
    rows = sum(vector.shape[1] for vector in vectors) // features
    return pl.pallas_call(
        pack_kernel,
        out_shape=jax.ShapeDtypeStruct((rows, features), jnp.float32),
        name="pack_rows",
    )(*vectors)


def row_major(matrix):
    return with_layout_constraint(matrix, Layout(major_to_minor=(0, 1)))


def column_parts(matrix, offset, width):
    step = matrix.shape[1] // 2
    return [lax.dynamic_slice_in_dim(matrix, t * step + offset, width, 1) for t in range(2)]


def grads_of(left, right, offset, width):
    return jnp.stack([row_major(tn(left, part).astype(jnp.bfloat16)) for part in column_parts(right, offset, width)])


def reduce_core(make, core):
    got = exchange(make(1 - core), 3)
    return add_low(make(core), got)


WINDOW = 32


def cut_kernel(cuts, place_ref, first_ref, *refs):
    summed, out, window, copied = refs[:6], refs[6], refs[7], refs[8]
    start = pl.multiple_of(place_ref[0], 16)
    copies = []
    for index, array in enumerate(summed):
        width = cuts[index + 1] - cuts[index]
        first_col = pl.multiple_of(place_ref[2] * width, 128)
        copies.append(
            pltpu.make_async_copy(
                array.at[pl.ds(start, WINDOW), pl.ds(first_col, width)],
                window.at[:, pl.ds(cuts[index], width)],
                copied.at[index],
            )
        )
        copies[-1].start()
    out[0] = first_ref[...].astype(jnp.float32)
    for copy in copies:
        copy.wait()
    rows = out.shape[1]
    row = jax.lax.broadcasted_iota(jnp.int32, (rows, WINDOW), 0)
    spot = jax.lax.broadcasted_iota(jnp.int32, (rows, WINDOW), 1)
    chosen = jnp.where(spot == row + place_ref[1], 1.0, 0.0).astype(jnp.bfloat16)
    out[1] = jnp.dot(chosen, window[...], preferred_element_type=jnp.float32)


def cut_rows(first_own, summed, dp_idx, tensor_idx, thin):
    features = summed[0].shape[0]
    start = jnp.minimum(dp_idx * thin // 16 * 16, features - WINDOW)
    place = jnp.stack([start, dp_idx * thin - start, tensor_idx]).astype(jnp.int32)
    cuts = [0]
    for array in summed:
        cuts.append(cuts[-1] + array.shape[1] // 2)
    vmem = pl.BlockSpec(memory_space=pltpu.VMEM)
    return pl.pallas_call(
        functools.partial(cut_kernel, tuple(cuts)),
        in_specs=[pl.BlockSpec(memory_space=pltpu.SMEM), vmem] + [pl.BlockSpec(memory_space=pltpu.HBM)] * 6,
        out_specs=vmem,
        out_shape=jax.ShapeDtypeStruct((LAYERS, 16, cuts[-1]), jnp.float32),
        scratch_shapes=[pltpu.VMEM((WINDOW, cuts[-1]), jnp.bfloat16), pltpu.SemaphoreType.DMA((6,))],
        compiler_params=pltpu.CompilerParams(vmem_limit_bytes=56 * 1024 * 1024),
        name="cut_rows",
    )(place, jnp.pad(first_own, ((0, 16 - thin), (0, 0))), *summed)


def split_heads(matrix):
    return matrix.reshape(matrix.shape[0], -1, HEAD).transpose(1, 0, 2)


def join_heads(matrix):
    return matrix.transpose(1, 0, 2).reshape(matrix.shape[1], -1)


def body(
    tokens,
    doc_lengths,
    qkv_weight,
    out_weight,
    inner_weight,
    down_weight,
    query_value_bias,
    hidden_bias,
    shifts,
    gains,
    cotangent,
):
    half_len, features = tokens.shape[1:]
    thin = qkv_weight.shape[3]
    head_cols = qkv_weight.shape[2]
    hidden_cols = inner_weight.shape[1]
    scale_factor = 1.0 / math.sqrt(HEAD)
    tensor_idx = lax.axis_index("tensor")
    dp_idx = lax.axis_index("dp")
    core = dp_idx & 1
    place = [tensor_idx * 2 + (dp_idx >> 5), (dp_idx >> 3) & 3, (dp_idx >> 1) & 3]

    weights = gather_weights(qkv_weight, out_weight, inner_weight, down_weight)
    bias_rows = jnp.concatenate(
        [query_value_bias.reshape(2 * LAYERS, head_cols), hidden_bias.reshape(-1, head_cols)], axis=0
    )
    bias_all = lax.all_gather(bias_rows, "tensor", axis=0, tiled=False)
    qv_bias = bias_all[:, : 2 * LAYERS].reshape(2, LAYERS, 2, head_cols)
    qv_bias = qv_bias.transpose(1, 2, 0, 3).reshape(LAYERS, 2, 2 * head_cols)
    hidden_full = bias_all[:, 2 * LAYERS :].reshape(2, LAYERS, hidden_cols)
    hidden_full = hidden_full.transpose(1, 0, 2).reshape(LAYERS, 2 * hidden_cols)

    position = jnp.arange(half_len, dtype=jnp.int32)
    mine_pos = position + tensor_idx * half_len
    key_pos = jnp.concatenate([mine_pos, position + (1 - tensor_idx) * half_len])
    first_end = doc_lengths[0, 0]
    second_end = first_end + doc_lengths[0, 1]

    def segment(pos):
        return (pos >= first_end).astype(jnp.int32) + (pos >= second_end).astype(jnp.int32)

    same_doc = segment(mine_pos)[:, None] == segment(key_pos)[None, :]

    hidden_state = tokens[0].astype(jnp.float32)
    rounded = tokens[0]
    saved_acts = []
    for layer_idx in range(LAYERS):
        query_w, key_value_w, out_w, inner_w, down_w = weights[layer_idx]
        rows = jnp.concatenate([rounded, swap_halves(rounded)], axis=0)
        query_b = (nn(rounded, query_w) + qv_bias[layer_idx, 0]).astype(jnp.bfloat16)
        key_b = nn(rows, key_value_w[0]).astype(jnp.bfloat16)
        value_b = (nn(rows, key_value_w[1]) + qv_bias[layer_idx, 1]).astype(jnp.bfloat16)
        query_h, key_h, value_h = split_heads(query_b), split_heads(key_b), split_heads(value_b)
        scores = (
            jnp.einsum("hqd,hkd->hqk", query_h, key_h, preferred_element_type=jnp.float32) * scale_factor
        )
        scores = jnp.where(same_doc[None], scores, masked_value)
        row_max = jnp.max(scores, axis=-1, keepdims=True)
        raised = jnp.exp(scores - row_max)
        row_total = jnp.sum(raised, axis=-1, keepdims=True)
        attn_probs = (raised / row_total).astype(jnp.bfloat16)
        log_total = row_max + jnp.log(row_total)
        attended = jnp.einsum("hqk,hkd->hqd", attn_probs, value_h, preferred_element_type=jnp.float32)
        attended_b = join_heads(attended.astype(jnp.bfloat16))
        branch = nt(attended_b, out_w)
        normed, normal_one, inverse_one = layer_norm(
            hidden_state + branch + shifts[layer_idx, 0], gains[layer_idx, 0], shifts[layer_idx, 1]
        )
        normed_low = normed.astype(jnp.bfloat16)
        pre_act = nn(normed_low, inner_w) + hidden_full[layer_idx]
        activated_b = exact_gelu(pre_act).astype(jnp.bfloat16)
        mlp_out = nt(activated_b, down_w)
        hidden_state, normal_two, inverse_two = layer_norm(
            normed + mlp_out + shifts[layer_idx, 2], gains[layer_idx, 1], shifts[layer_idx, 3]
        )
        saved_acts.append(
            (rows, query_h, key_h, value_h, log_total, attended_b, normal_one, inverse_one, normed_low,
             pre_act, activated_b, normal_two, inverse_two)
        )
        rounded = hidden_state.astype(jnp.bfloat16)
    output = hidden_state

    def backward(layer_idx, state_grad):
        query_w, key_value_w, out_w, inner_w, down_w = weights[layer_idx]
        (rows, query_h, key_h, value_h, log_total, attended_b, normal_one, inverse_one, normed_low,
         pre_act, activated_b, normal_two, inverse_two) = saved_acts[layer_idx]
        pre_two_grad = norm_back(state_grad, normal_two, inverse_two, gains[layer_idx, 1])
        gain_two = jnp.sum(state_grad * normal_two, axis=0, keepdims=True)
        beta_two = jnp.sum(state_grad, axis=0, keepdims=True)
        shift_two = jnp.sum(pre_two_grad, axis=0, keepdims=True)
        mlp_grad_b = pre_two_grad.astype(jnp.bfloat16)
        half_hidden = hidden_cols // 2
        if layer_idx > 0:
            down_local = tn(mlp_grad_b, activated_b).astype(jnp.bfloat16)
        else:
            down_part = reduce_core(
                lambda side: grads_of(mlp_grad_b, activated_b, side * half_hidden, half_hidden), core
            )
        activated_grad = nn(mlp_grad_b, down_w)
        _, gelu_back = jax.vjp(exact_gelu, pre_act)
        pre_act_grad = gelu_back(activated_grad)[0].astype(jnp.bfloat16)
        hidden_part = jnp.sum(pre_act_grad.astype(jnp.float32), axis=0, keepdims=True)
        if layer_idx > 0:
            inner_local = tn(normed_low, pre_act_grad).astype(jnp.bfloat16)
        else:
            inner_part = reduce_core(
                lambda side: grads_of(normed_low, pre_act_grad, side * half_hidden, half_hidden), core
            )
            wide_parts = [inner_part, down_part]
        normed_grad = pre_two_grad + nt(pre_act_grad, inner_w)
        pre_one_grad = norm_back(normed_grad, normal_one, inverse_one, gains[layer_idx, 0])
        gain_one = jnp.sum(normed_grad * normal_one, axis=0, keepdims=True)
        beta_one = jnp.sum(normed_grad, axis=0, keepdims=True)
        shift_one = jnp.sum(pre_one_grad, axis=0, keepdims=True)
        attn_grad_b = pre_one_grad.astype(jnp.bfloat16)
        if layer_idx > 0:
            out_local = tn(attn_grad_b, attended_b).astype(jnp.bfloat16)
        attended_grad = nn(attn_grad_b, out_w).astype(jnp.bfloat16)
        attended_grad_h = split_heads(attended_grad)
        scores = (
            jnp.einsum("hqd,hkd->hqk", query_h, key_h, preferred_element_type=jnp.float32) * scale_factor
        )
        scores = jnp.where(same_doc[None], scores, masked_value)
        probs_full = jnp.exp(scores - log_total)
        probs_low = probs_full.astype(jnp.bfloat16)
        value_grad = jnp.einsum("hqk,hqd->hkd", probs_low, attended_grad_h, preferred_element_type=jnp.float32)
        prob_grad = jnp.einsum("hqd,hkd->hqk", attended_grad_h, value_h, preferred_element_type=jnp.float32)
        row_dot = jnp.sum(prob_grad * probs_full, axis=-1, keepdims=True)
        score_grad = (probs_full * (prob_grad - row_dot)).astype(jnp.bfloat16)
        query_grad = (
            jnp.einsum("hqk,hkd->hqd", score_grad, key_h, preferred_element_type=jnp.float32) * scale_factor
        )
        key_grad = (
            jnp.einsum("hqk,hqd->hkd", score_grad, query_h, preferred_element_type=jnp.float32) * scale_factor
        )
        query_grad_b = join_heads(query_grad.astype(jnp.bfloat16))
        key_grad_b = join_heads(key_grad.astype(jnp.bfloat16))
        value_grad_b = join_heads(value_grad.astype(jnp.bfloat16))
        qv_part = [
            jnp.sum(query_grad_b.astype(jnp.float32), axis=0, keepdims=True),
            jnp.sum(value_grad_b.astype(jnp.float32), axis=0, keepdims=True),
        ]
        if layer_idx > 0:
            query_local = tn(rows[:half_len], query_grad_b).astype(jnp.bfloat16)
            key_local = tn(rows, key_grad_b).astype(jnp.bfloat16)
            value_local = tn(rows, value_grad_b).astype(jnp.bfloat16)
            locals_all = tuple(
                row_major(part)
                for part in (query_local, key_local, value_local, out_local, inner_local, down_local)
            )
        else:
            padding = ((0, half_len), (0, 0))
            query_pad, attn_pad, attended_pad = (
                jnp.pad(v, padding) for v in (query_grad_b, attn_grad_b, attended_b)
            )

            def first_grads(side):
                return grads_of(rows, jnp.where(side == 0, query_pad, value_grad_b), 0, head_cols)

            def second_grads(side):
                left = jnp.where(side == 0, rows, attn_pad)
                return grads_of(left, jnp.where(side == 0, key_grad_b, attended_pad), 0, head_cols)

            attn_parts = [reduce_core(first_grads, core), reduce_core(second_grads, core)]
        both = nt(key_grad_b, key_value_w[0]) + nt(value_grad_b, key_value_w[1])
        theirs = swap_halves(both[half_len:].astype(jnp.bfloat16))
        state_grad = (
            pre_one_grad
            + nt(query_grad_b, query_w)
            + both[:half_len]
            + theirs.astype(jnp.float32)
        )
        sums = [shift_one, beta_one, shift_two, beta_two, gain_one, gain_two, *qv_part, hidden_part]
        if layer_idx > 0:
            return state_grad, sums, locals_all
        return state_grad, sums, (wide_parts, attn_parts)

    second_grad, second_sums, second_parts = backward(1, cotangent[0])
    second_parts, second_grad = lax.optimization_barrier((second_parts, second_grad))
    summed = lax.psum(second_parts, ALL)

    def first_layer(state_grad, second_sums):
        state_grad, sums, (wide_parts, attn_parts) = backward(0, state_grad)
        sums, second_sums, attn_parts = lax.optimization_barrier((sums, second_sums, attn_parts))
        small = pack_rows(sums + second_sums, features)
        wide = scatter_rounds(wide_parts, place, (1, 2, 0))
        attn = scatter_rounds(attn_parts, place, (0, 1, 2))
        tiny = sum_rounds(small)
        state = lax.optimization_barrier((next(wide), next(attn), next(tiny)))
        for _ in range(5):
            state = lax.optimization_barrier((wide.send(state[0]), attn.send(state[1]), tiny.send(state[2])))
        wide_parts, attn_parts, small = state
        first_rows = jnp.concatenate(
            [attn_parts[0].reshape(2 * thin, -1), wide_parts[0].reshape(2 * thin, -1)], axis=1
        )
        theirs = exchange(lax.dynamic_slice_in_dim(first_rows, (1 - core) * thin, thin, 0), 3)
        mine = lax.dynamic_slice_in_dim(first_rows, core * thin, thin, 0)
        low_side = jnp.where(core == 0, mine, theirs).reshape(thin, 3, -1)
        high_side = jnp.where(core == 0, theirs, mine).reshape(thin, 3, -1)
        first_own = jnp.concatenate([low_side, high_side], axis=2).reshape(thin, -1)
        return state_grad, first_own, tiny.send(small)

    def no_layer(state_grad, second_sums):
        first_own = jnp.zeros((thin, 4 * head_cols + 2 * hidden_cols), jnp.bfloat16)
        return state_grad, first_own, jnp.zeros((LAYERS * 12, features), jnp.float32)

    state_grad, first_own, small = lax.cond(
        doc_lengths[0, 0] >= 0, first_layer, no_layer, second_grad, second_sums
    )
    small_sum = small.reshape(LAYERS, -1)
    both_own = cut_rows(first_own, summed, dp_idx, tensor_idx, thin)[:, :thin]

    def result(start, stop):
        return both_own[:, :, start:stop].transpose(0, 2, 1)

    qkv_result = both_own[:, :, : 3 * head_cols].reshape(LAYERS, thin, 3, head_cols).transpose(0, 2, 3, 1)
    out_result = result(3 * head_cols, 4 * head_cols)
    inner_result = result(4 * head_cols, 4 * head_cols + hidden_cols)
    down_result = result(4 * head_cols + hidden_cols, 4 * head_cols + 2 * hidden_cols)
    shift_total = small_sum[:, : 4 * features].reshape(LAYERS, 4, features)
    gain_total = small_sum[:, 4 * features : 6 * features].reshape(LAYERS, 2, features)
    qv_total = lax.dynamic_slice_in_dim(
        small_sum[:, 6 * features : 8 * features].reshape(LAYERS, 2, features), tensor_idx * head_cols, head_cols, 2
    )
    hidden_total = lax.dynamic_slice_in_dim(small_sum[:, 8 * features :], tensor_idx * hidden_cols, hidden_cols, 1)
    return (
        output[None],
        state_grad[None],
        qkv_result,
        out_result,
        inner_result,
        down_result,
        qv_total,
        hidden_total,
        shift_total,
        gain_total,
    )


def solution(mesh):
    in_specs = (
        P("dp", "tensor", None),
        P("dp", None),
        P(None, None, "tensor", "dp"),
        P(None, "tensor", "dp"),
        P(None, "tensor", "dp"),
        P(None, "tensor", "dp"),
        P(None, None, "tensor"),
        P(None, "tensor"),
        P(),
        P(),
        P("dp", "tensor", None),
    )
    out_specs = (
        P("dp", "tensor", None),
        P("dp", "tensor", None),
        P(None, None, "tensor", "dp"),
        P(None, "tensor", "dp"),
        P(None, "tensor", "dp"),
        P(None, "tensor", "dp"),
        P(None, None, "tensor"),
        P(None, "tensor"),
        P(),
        P(),
    )
    return jax.shard_map(body, mesh=mesh, in_specs=in_specs, out_specs=out_specs, check_vma=False)
```

```python
import functools
import math

import jax
import jax.numpy as jnp
from jax import lax
from jax.experimental import pallas as pl
from jax.experimental.layout import Layout, with_layout_constraint
from jax.experimental.pallas import tpu as pltpu
from jax.sharding import PartitionSpec as P

HEAD = 64
LAYERS = 2
ALL = ("tensor", "dp")


epsilon = 1e-06
masked_value = -1e30


def layer_norm(values, gain_vec, shift_vec):
    center = values - jnp.mean(values, axis=-1, keepdims=True)
    variance = jnp.mean(center * center, axis=-1, keepdims=True)
    inverse = lax.rsqrt(variance + epsilon)
    normal = center * inverse
    return normal * gain_vec + shift_vec, normal, inverse


def norm_back(grad, normal, inverse, gain_vec):
    scaled = grad * gain_vec
    mean_one = jnp.mean(scaled, axis=-1, keepdims=True)
    mean_two = jnp.mean(scaled * normal, axis=-1, keepdims=True)
    return inverse * (scaled - mean_one - normal * mean_two)


def exact_gelu(values):
    return jax.nn.gelu(values, approximate=False)


def nn(left, right):
    return lax.dot_general(left, right, (((1,), (0,)), ((), ())), preferred_element_type=jnp.float32)


def nt(left, right):
    return lax.dot_general(left, right, (((1,), (1,)), ((), ())), preferred_element_type=jnp.float32)


def tn(left, right):
    return lax.dot_general(left, right, (((0,), (0,)), ((), ())), preferred_element_type=jnp.float32)


def swap_halves(values):
    return lax.ppermute(values, "tensor", [(0, 1), (1, 0)])


def unpack_kernel(order_ref, packed_ref, query_ref, key_value_ref, out_ref, inner_ref, down_ref):
    picked = jnp.dot(order_ref[...], packed_ref[...], preferred_element_type=jnp.float32)
    picked = picked.astype(jnp.bfloat16)
    rows, cols = query_ref.shape
    hidden = inner_ref.shape[1] // 2
    query_ref[...] = picked[:rows, :cols]
    key_value_ref[0] = picked[:rows, cols : 2 * cols]
    key_value_ref[1] = picked[:rows, 2 * cols : 3 * cols]
    out_ref[...] = picked[:rows, 3 * cols : 4 * cols]
    inner_ref[:, :hidden] = picked[:rows, 4 * cols :]
    inner_ref[:, hidden:] = picked[rows:, :hidden]
    down_ref[...] = picked[rows:, hidden:]


def unpack_layer(gathered, layer_idx, thin, features, cols, hidden):
    group = 8
    tall = 2 * thin * group
    flat = thin * group
    width = gathered.shape[1] // LAYERS
    blocks = features // flat
    spot = jnp.arange(tall, dtype=jnp.int32)
    half = spot // flat
    source = (spot % flat) // thin * (2 * thin) + half * thin + spot % thin
    order = (source[:, None] == jnp.arange(tall, dtype=jnp.int32)[None, :]).astype(jnp.bfloat16)
    return pl.pallas_call(
        unpack_kernel,
        grid=(2, blocks),
        in_specs=[
            pl.BlockSpec((tall, tall), lambda t, r: (0, 0)),
            pl.BlockSpec((tall, width), lambda t, r: (t * blocks + r, layer_idx)),
        ],
        out_specs=[
            pl.BlockSpec((flat, cols), lambda t, r: (r, t)),
            pl.BlockSpec((2, flat, cols), lambda t, r: (0, r, t)),
            pl.BlockSpec((flat, cols), lambda t, r: (r, t)),
            pl.BlockSpec((flat, hidden), lambda t, r: (r, t)),
            pl.BlockSpec((flat, hidden), lambda t, r: (r, t)),
        ],
        out_shape=[
            jax.ShapeDtypeStruct((features, 2 * cols), jnp.bfloat16),
            jax.ShapeDtypeStruct((2, features, 2 * cols), jnp.bfloat16),
            jax.ShapeDtypeStruct((features, 2 * cols), jnp.bfloat16),
            jax.ShapeDtypeStruct((features, 2 * hidden), jnp.bfloat16),
            jax.ShapeDtypeStruct((features, 2 * hidden), jnp.bfloat16),
        ],
        compiler_params=pltpu.CompilerParams(vmem_limit_bytes=40 * 1024 * 1024),
        name="unpack_layer",
    )(order, gathered)


def gather_weights(qkv_weight, out_weight, inner_weight, down_weight):
    layers = qkv_weight.shape[0]
    thin = qkv_weight.shape[3]
    cols, hidden = out_weight.shape[1], inner_weight.shape[1]
    piece = jnp.concatenate(
        [qkv_weight.reshape(layers, -1, thin), out_weight, inner_weight, down_weight], axis=1
    )
    width = piece.shape[1]
    piece = piece.reshape(layers, 2, width // 2, thin).transpose(1, 3, 0, 2).reshape(2 * thin, width)
    whole = lax.all_gather(piece, ALL, axis=0, tiled=True)
    features = whole.shape[0] // 4
    return [unpack_layer(whole, layer, thin, features, cols, hidden) for layer in range(layers)]


def coords(flat):
    dp = flat >> 1
    return [(flat & 1) * 2 + (dp >> 5), (dp >> 3) & 3, (dp >> 1) & 3, dp & 1]


def flat_index(x, z, y, core):
    return ((((x & 1) * 4 + z) * 4 + y) * 2 + core) * 2 + (x >> 1)


def partner(pos, kind):
    return pos ^ 1 if kind == 0 else (pos ^ 1) ^ 2


def exchange(values, axis, kind=0):
    pairs = []
    for flat in range(128):
        place = coords(flat)
        place[axis] = place[axis] ^ 1 if axis == 3 else partner(place[axis], kind)
        pairs.append((flat, flat_index(*place)))
    return lax.ppermute(values, ("dp", "tensor"), pairs)


def add_low(left, right):
    return (left.astype(jnp.float32) + right.astype(jnp.float32)).astype(jnp.bfloat16)


def pick(values, index, dim):
    return lax.dynamic_slice_in_dim(values, index, 1, dim)


def halve_first(values, place, axis, kind):
    me = place[axis]
    first, second = partner(me, kind), partner(me, 1 - kind)
    sent = jnp.concatenate(
        [pick(values, first, axis), pick(values, partner(first, 1 - kind), axis)], axis=axis
    )
    got = exchange(sent, axis, kind)
    kept = jnp.concatenate([pick(values, me, axis), pick(values, second, axis)], axis=axis)
    return add_low(kept, got)


def halve_second(kept, axis, kind):
    last = exchange(lax.slice_in_dim(kept, 1, 2, axis=axis), axis, 1 - kind)
    return add_low(lax.slice_in_dim(kept, 0, 1, axis=axis), last)


def scatter_rounds(parts, place, order):
    parts = [part.reshape(4, 4, 4, -1, part.shape[-1]) for part in parts]
    for step, axis in enumerate(order):
        if step == 1:
            parts = [jnp.concatenate(parts, axis=-1)]
        parts = yield [halve_first(part, place, axis, kind) for kind, part in enumerate(parts)]
        parts = yield [halve_second(part, axis, kind) for kind, part in enumerate(parts)]


def sum_rounds(values):
    values = yield values + exchange(values, 3)
    for axis in range(3):
        for kind in range(2):
            values = yield values + exchange(values, axis, kind)


def pack_kernel(*refs):
    packed = refs[-1]
    row = 0
    for ref in refs[:-1]:
        for part in range(ref.shape[1] // packed.shape[1]):
            packed[row : row + 1, :] = ref[:, part * packed.shape[1] : (part + 1) * packed.shape[1]]
            row += 1


def pack_rows(vectors, features):
    rows = sum(vector.shape[1] for vector in vectors) // features
    return pl.pallas_call(
        pack_kernel,
        out_shape=jax.ShapeDtypeStruct((rows, features), jnp.float32),
        name="pack_rows",
    )(*vectors)


def row_major(matrix):
    return with_layout_constraint(matrix, Layout(major_to_minor=(0, 1)))


def column_parts(matrix, offset, width):
    step = matrix.shape[1] // 2
    return [lax.dynamic_slice_in_dim(matrix, t * step + offset, width, 1) for t in range(2)]


def grads_of(left, right, offset, width):
    return jnp.stack([row_major(tn(left, part).astype(jnp.bfloat16)) for part in column_parts(right, offset, width)])


def reduce_core(make, core):
    got = exchange(make(1 - core), 3)
    return add_low(make(core), got)


WINDOW = 32


def cut_kernel(cuts, place_ref, first_ref, *refs):
    summed, out, window, copied = refs[:6], refs[6], refs[7], refs[8]
    start = pl.multiple_of(place_ref[0], 16)
    copies = []
    for index, array in enumerate(summed):
        width = cuts[index + 1] - cuts[index]
        first_col = pl.multiple_of(place_ref[2] * width, 128)
        copies.append(
            pltpu.make_async_copy(
                array.at[pl.ds(start, WINDOW), pl.ds(first_col, width)],
                window.at[:, pl.ds(cuts[index], width)],
                copied.at[index],
            )
        )
        copies[-1].start()
    out[0] = first_ref[...].astype(jnp.float32)
    for copy in copies:
        copy.wait()
    rows = out.shape[1]
    row = jax.lax.broadcasted_iota(jnp.int32, (rows, WINDOW), 0)
    spot = jax.lax.broadcasted_iota(jnp.int32, (rows, WINDOW), 1)
    chosen = jnp.where(spot == row + place_ref[1], 1.0, 0.0).astype(jnp.bfloat16)
    out[1] = jnp.dot(chosen, window[...], preferred_element_type=jnp.float32)


def cut_rows(first_own, summed, dp_idx, tensor_idx, thin):
    features = summed[0].shape[0]
    start = jnp.minimum(dp_idx * thin // 16 * 16, features - WINDOW)
    place = jnp.stack([start, dp_idx * thin - start, tensor_idx]).astype(jnp.int32)
    cuts = [0]
    for array in summed:
        cuts.append(cuts[-1] + array.shape[1] // 2)
    vmem = pl.BlockSpec(memory_space=pltpu.VMEM)
    return pl.pallas_call(
        functools.partial(cut_kernel, tuple(cuts)),
        in_specs=[pl.BlockSpec(memory_space=pltpu.SMEM), vmem] + [pl.BlockSpec(memory_space=pltpu.HBM)] * 6,
        out_specs=vmem,
        out_shape=jax.ShapeDtypeStruct((LAYERS, 16, cuts[-1]), jnp.float32),
        scratch_shapes=[pltpu.VMEM((WINDOW, cuts[-1]), jnp.bfloat16), pltpu.SemaphoreType.DMA((6,))],
        compiler_params=pltpu.CompilerParams(vmem_limit_bytes=56 * 1024 * 1024),
        name="cut_rows",
    )(place, jnp.pad(first_own, ((0, 16 - thin), (0, 0))), *summed)


def split_heads(matrix):
    return matrix.reshape(matrix.shape[0], -1, HEAD).transpose(1, 0, 2)


def join_heads(matrix):
    return matrix.transpose(1, 0, 2).reshape(matrix.shape[1], -1)


def body(
    tokens,
    doc_lengths,
    qkv_weight,
    out_weight,
    inner_weight,
    down_weight,
    query_value_bias,
    hidden_bias,
    shifts,
    gains,
    cotangent,
):
    half_len, features = tokens.shape[1:]
    thin = qkv_weight.shape[3]
    head_cols = qkv_weight.shape[2]
    hidden_cols = inner_weight.shape[1]
    scale_factor = 1.0 / math.sqrt(HEAD)
    tensor_idx = lax.axis_index("tensor")
    dp_idx = lax.axis_index("dp")
    core = dp_idx & 1
    place = [tensor_idx * 2 + (dp_idx >> 5), (dp_idx >> 3) & 3, (dp_idx >> 1) & 3]

    weights = gather_weights(qkv_weight, out_weight, inner_weight, down_weight)
    bias_rows = jnp.concatenate(
        [query_value_bias.reshape(2 * LAYERS, head_cols), hidden_bias.reshape(-1, head_cols)], axis=0
    )
    bias_all = lax.all_gather(bias_rows, "tensor", axis=0, tiled=False)
    qv_bias = bias_all[:, : 2 * LAYERS].reshape(2, LAYERS, 2, head_cols)
    qv_bias = qv_bias.transpose(1, 2, 0, 3).reshape(LAYERS, 2, 2 * head_cols)
    hidden_full = bias_all[:, 2 * LAYERS :].reshape(2, LAYERS, hidden_cols)
    hidden_full = hidden_full.transpose(1, 0, 2).reshape(LAYERS, 2 * hidden_cols)

    position = jnp.arange(half_len, dtype=jnp.int32)
    mine_pos = position + tensor_idx * half_len
    key_pos = jnp.concatenate([mine_pos, position + (1 - tensor_idx) * half_len])
    first_end = doc_lengths[0, 0]
    second_end = first_end + doc_lengths[0, 1]

    def segment(pos):
        return (pos >= first_end).astype(jnp.int32) + (pos >= second_end).astype(jnp.int32)

    same_doc = segment(mine_pos)[:, None] == segment(key_pos)[None, :]

    hidden_state = tokens[0].astype(jnp.float32)
    rounded = tokens[0]
    saved_acts = []
    for layer_idx in range(LAYERS):
        query_w, key_value_w, out_w, inner_w, down_w = weights[layer_idx]
        rows = jnp.concatenate([rounded, swap_halves(rounded)], axis=0)
        query_b = (nn(rounded, query_w) + qv_bias[layer_idx, 0]).astype(jnp.bfloat16)
        key_b = nn(rows, key_value_w[0]).astype(jnp.bfloat16)
        value_b = (nn(rows, key_value_w[1]) + qv_bias[layer_idx, 1]).astype(jnp.bfloat16)
        query_h, key_h, value_h = split_heads(query_b), split_heads(key_b), split_heads(value_b)
        scores = (
            jnp.einsum("hqd,hkd->hqk", query_h, key_h, preferred_element_type=jnp.float32) * scale_factor
        )
        scores = jnp.where(same_doc[None], scores, masked_value)
        row_max = jnp.max(scores, axis=-1, keepdims=True)
        raised = jnp.exp(scores - row_max)
        row_total = jnp.sum(raised, axis=-1, keepdims=True)
        attn_probs = (raised / row_total).astype(jnp.bfloat16)
        log_total = row_max + jnp.log(row_total)
        attended = jnp.einsum("hqk,hkd->hqd", attn_probs, value_h, preferred_element_type=jnp.float32)
        attended_b = join_heads(attended.astype(jnp.bfloat16))
        branch = nt(attended_b, out_w)
        normed, normal_one, inverse_one = layer_norm(
            hidden_state + branch + shifts[layer_idx, 0], gains[layer_idx, 0], shifts[layer_idx, 1]
        )
        normed_low = normed.astype(jnp.bfloat16)
        pre_act = nn(normed_low, inner_w) + hidden_full[layer_idx]
        activated_b = exact_gelu(pre_act).astype(jnp.bfloat16)
        mlp_out = nt(activated_b, down_w)
        hidden_state, normal_two, inverse_two = layer_norm(
            normed + mlp_out + shifts[layer_idx, 2], gains[layer_idx, 1], shifts[layer_idx, 3]
        )
        saved_acts.append(
            (rows, query_h, key_h, value_h, log_total, attended_b, normal_one, inverse_one, normed_low,
             pre_act, activated_b, normal_two, inverse_two)
        )
        rounded = hidden_state.astype(jnp.bfloat16)
    output = hidden_state

    def backward(layer_idx, state_grad):
        query_w, key_value_w, out_w, inner_w, down_w = weights[layer_idx]
        (rows, query_h, key_h, value_h, log_total, attended_b, normal_one, inverse_one, normed_low,
         pre_act, activated_b, normal_two, inverse_two) = saved_acts[layer_idx]
        pre_two_grad = norm_back(state_grad, normal_two, inverse_two, gains[layer_idx, 1])
        gain_two = jnp.sum(state_grad * normal_two, axis=0, keepdims=True)
        beta_two = jnp.sum(state_grad, axis=0, keepdims=True)
        shift_two = jnp.sum(pre_two_grad, axis=0, keepdims=True)
        mlp_grad_b = pre_two_grad.astype(jnp.bfloat16)
        half_hidden = hidden_cols // 2
        if layer_idx > 0:
            down_local = tn(mlp_grad_b, activated_b).astype(jnp.bfloat16)
        else:
            down_part = reduce_core(
                lambda side: grads_of(mlp_grad_b, activated_b, side * half_hidden, half_hidden), core
            )
        activated_grad = nn(mlp_grad_b, down_w)
        _, gelu_back = jax.vjp(exact_gelu, pre_act)
        pre_act_grad = gelu_back(activated_grad)[0].astype(jnp.bfloat16)
        hidden_part = jnp.sum(pre_act_grad.astype(jnp.float32), axis=0, keepdims=True)
        if layer_idx > 0:
            inner_local = tn(normed_low, pre_act_grad).astype(jnp.bfloat16)
        else:
            inner_part = reduce_core(
                lambda side: grads_of(normed_low, pre_act_grad, side * half_hidden, half_hidden), core
            )
            wide_parts = [inner_part, down_part]
        normed_grad = pre_two_grad + nt(pre_act_grad, inner_w)
        pre_one_grad = norm_back(normed_grad, normal_one, inverse_one, gains[layer_idx, 0])
        gain_one = jnp.sum(normed_grad * normal_one, axis=0, keepdims=True)
        beta_one = jnp.sum(normed_grad, axis=0, keepdims=True)
        shift_one = jnp.sum(pre_one_grad, axis=0, keepdims=True)
        attn_grad_b = pre_one_grad.astype(jnp.bfloat16)
        if layer_idx > 0:
            out_local = tn(attn_grad_b, attended_b).astype(jnp.bfloat16)
        attended_grad = nn(attn_grad_b, out_w).astype(jnp.bfloat16)
        attended_grad_h = split_heads(attended_grad)
        scores = (
            jnp.einsum("hqd,hkd->hqk", query_h, key_h, preferred_element_type=jnp.float32) * scale_factor
        )
        scores = jnp.where(same_doc[None], scores, masked_value)
        probs_full = jnp.exp(scores - log_total)
        probs_low = probs_full.astype(jnp.bfloat16)
        value_grad = jnp.einsum("hqk,hqd->hkd", probs_low, attended_grad_h, preferred_element_type=jnp.float32)
        prob_grad = jnp.einsum("hqd,hkd->hqk", attended_grad_h, value_h, preferred_element_type=jnp.float32)
        row_dot = jnp.sum(prob_grad * probs_full, axis=-1, keepdims=True)
        score_grad = (probs_full * (prob_grad - row_dot)).astype(jnp.bfloat16)
        query_grad = (
            jnp.einsum("hqk,hkd->hqd", score_grad, key_h, preferred_element_type=jnp.float32) * scale_factor
        )
        key_grad = (
            jnp.einsum("hqk,hqd->hkd", score_grad, query_h, preferred_element_type=jnp.float32) * scale_factor
        )
        query_grad_b = join_heads(query_grad.astype(jnp.bfloat16))
        key_grad_b = join_heads(key_grad.astype(jnp.bfloat16))
        value_grad_b = join_heads(value_grad.astype(jnp.bfloat16))
        qv_part = [
            jnp.sum(query_grad_b.astype(jnp.float32), axis=0, keepdims=True),
            jnp.sum(value_grad_b.astype(jnp.float32), axis=0, keepdims=True),
        ]
        if layer_idx > 0:
            query_local = tn(rows[:half_len], query_grad_b).astype(jnp.bfloat16)
            key_local = tn(rows, key_grad_b).astype(jnp.bfloat16)
            value_local = tn(rows, value_grad_b).astype(jnp.bfloat16)
            locals_all = tuple(
                row_major(part)
                for part in (query_local, key_local, value_local, out_local, inner_local, down_local)
            )
        else:
            padding = ((0, half_len), (0, 0))
            query_pad, attn_pad, attended_pad = (
                jnp.pad(v, padding) for v in (query_grad_b, attn_grad_b, attended_b)
            )

            def first_grads(side):
                return grads_of(rows, jnp.where(side == 0, query_pad, value_grad_b), 0, head_cols)

            def second_grads(side):
                left = jnp.where(side == 0, rows, attn_pad)
                return grads_of(left, jnp.where(side == 0, key_grad_b, attended_pad), 0, head_cols)

            attn_parts = [reduce_core(first_grads, core), reduce_core(second_grads, core)]
        both = nt(key_grad_b, key_value_w[0]) + nt(value_grad_b, key_value_w[1])
        theirs = swap_halves(both[half_len:].astype(jnp.bfloat16))
        state_grad = (
            pre_one_grad
            + nt(query_grad_b, query_w)
            + both[:half_len]
            + theirs.astype(jnp.float32)
        )
        sums = [shift_one, beta_one, shift_two, beta_two, gain_one, gain_two, *qv_part, hidden_part]
        if layer_idx > 0:
            return state_grad, sums, locals_all
        return state_grad, sums, (wide_parts, attn_parts)

    second_grad, second_sums, second_parts = backward(1, cotangent[0])
    second_parts, second_grad = lax.optimization_barrier((second_parts, second_grad))
    summed = lax.psum(second_parts, ALL)

    def first_layer(state_grad, second_sums):
        state_grad, sums, (wide_parts, attn_parts) = backward(0, state_grad)
        wide = scatter_rounds(wide_parts, place, (1, 2, 0))
        wide_parts, attn_parts = lax.optimization_barrier((next(wide), attn_parts))
        attn = scatter_rounds(attn_parts, place, (0, 1, 2))
        wide_parts, attn_parts = lax.optimization_barrier((wide.send(wide_parts), next(attn)))
        tiny = sum_rounds(pack_rows(sums + second_sums, features))
        small = next(tiny)
        wide_parts, attn_parts, small = lax.optimization_barrier(
            (wide.send(wide_parts), attn.send(attn_parts), small)
        )
        wide_parts, attn_parts, small, state_grad = lax.optimization_barrier(
            (wide.send(wide_parts), attn.send(attn_parts), tiny.send(small), state_grad)
        )
        for _ in range(2):
            wide_parts, attn_parts, small = lax.optimization_barrier(
                (wide.send(wide_parts), attn.send(attn_parts), tiny.send(small))
            )
        attn_parts, small = lax.optimization_barrier((attn.send(attn_parts), tiny.send(small)))
        small = tiny.send(small)
        first_rows = jnp.concatenate(
            [attn_parts[0].reshape(2 * thin, -1), wide_parts[0].reshape(2 * thin, -1)], axis=1
        )
        theirs = exchange(lax.dynamic_slice_in_dim(first_rows, (1 - core) * thin, thin, 0), 3)
        mine = lax.dynamic_slice_in_dim(first_rows, core * thin, thin, 0)
        low_side = jnp.where(core == 0, mine, theirs).reshape(thin, 3, -1)
        high_side = jnp.where(core == 0, theirs, mine).reshape(thin, 3, -1)
        first_own = jnp.concatenate([low_side, high_side], axis=2).reshape(thin, -1)
        return state_grad, first_own, tiny.send(small)

    def no_layer(state_grad, second_sums):
        first_own = jnp.zeros((thin, 4 * head_cols + 2 * hidden_cols), jnp.bfloat16)
        return state_grad, first_own, jnp.zeros((LAYERS * 12, features), jnp.float32)

    state_grad, first_own, small = lax.cond(
        doc_lengths[0, 0] >= 0, first_layer, no_layer, second_grad, second_sums
    )
    small_sum = small.reshape(LAYERS, -1)
    both_own = cut_rows(first_own, summed, dp_idx, tensor_idx, thin)[:, :thin]

    def result(start, stop):
        return both_own[:, :, start:stop].transpose(0, 2, 1)

    qkv_result = both_own[:, :, : 3 * head_cols].reshape(LAYERS, thin, 3, head_cols).transpose(0, 2, 3, 1)
    out_result = result(3 * head_cols, 4 * head_cols)
    inner_result = result(4 * head_cols, 4 * head_cols + hidden_cols)
    down_result = result(4 * head_cols + hidden_cols, 4 * head_cols + 2 * hidden_cols)
    shift_total = small_sum[:, : 4 * features].reshape(LAYERS, 4, features)
    gain_total = small_sum[:, 4 * features : 6 * features].reshape(LAYERS, 2, features)
    qv_total = lax.dynamic_slice_in_dim(
        small_sum[:, 6 * features : 8 * features].reshape(LAYERS, 2, features), tensor_idx * head_cols, head_cols, 2
    )
    hidden_total = lax.dynamic_slice_in_dim(small_sum[:, 8 * features :], tensor_idx * hidden_cols, hidden_cols, 1)
    return (
        output[None],
        state_grad[None],
        qkv_result,
        out_result,
        inner_result,
        down_result,
        qv_total,
        hidden_total,
        shift_total,
        gain_total,
    )


def solution(mesh):
    in_specs = (
        P("dp", "tensor", None),
        P("dp", None),
        P(None, None, "tensor", "dp"),
        P(None, "tensor", "dp"),
        P(None, "tensor", "dp"),
        P(None, "tensor", "dp"),
        P(None, None, "tensor"),
        P(None, "tensor"),
        P(),
        P(),
        P("dp", "tensor", None),
    )
    out_specs = (
        P("dp", "tensor", None),
        P("dp", "tensor", None),
        P(None, None, "tensor", "dp"),
        P(None, "tensor", "dp"),
        P(None, "tensor", "dp"),
        P(None, "tensor", "dp"),
        P(None, None, "tensor"),
        P(None, "tensor"),
        P(),
        P(),
    )
    return jax.shard_map(body, mesh=mesh, in_specs=in_specs, out_specs=out_specs, check_vma=False)
```

```python
import functools
import math

import jax
import jax.numpy as jnp
from jax import lax
from jax.experimental import pallas as pl
from jax.experimental.layout import Layout, with_layout_constraint
from jax.experimental.pallas import tpu as pltpu
from jax.sharding import PartitionSpec as P

HEAD = 64
LAYERS = 2
ALL = ("tensor", "dp")


epsilon = 1e-06
masked_value = -1e30


def layer_norm(values, gain_vec, shift_vec):
    center = values - jnp.mean(values, axis=-1, keepdims=True)
    variance = jnp.mean(center * center, axis=-1, keepdims=True)
    inverse = lax.rsqrt(variance + epsilon)
    normal = center * inverse
    return normal * gain_vec + shift_vec, normal, inverse


def norm_back(grad, normal, inverse, gain_vec):
    scaled = grad * gain_vec
    mean_one = jnp.mean(scaled, axis=-1, keepdims=True)
    mean_two = jnp.mean(scaled * normal, axis=-1, keepdims=True)
    return inverse * (scaled - mean_one - normal * mean_two)


def exact_gelu(values):
    return jax.nn.gelu(values, approximate=False)


def nn(left, right):
    return lax.dot_general(left, right, (((1,), (0,)), ((), ())), preferred_element_type=jnp.float32)


def nt(left, right):
    return lax.dot_general(left, right, (((1,), (1,)), ((), ())), preferred_element_type=jnp.float32)


def tn(left, right):
    return lax.dot_general(left, right, (((0,), (0,)), ((), ())), preferred_element_type=jnp.float32)


def swap_halves(values):
    return lax.ppermute(values, "tensor", [(0, 1), (1, 0)])


def unpack_kernel(order_ref, packed_ref, query_ref, key_value_ref, out_ref, inner_ref, down_ref):
    picked = jnp.dot(order_ref[...], packed_ref[...], preferred_element_type=jnp.float32)
    picked = picked.astype(jnp.bfloat16)
    rows, cols = query_ref.shape
    hidden = inner_ref.shape[1] // 2
    query_ref[...] = picked[:rows, :cols]
    key_value_ref[0] = picked[:rows, cols : 2 * cols]
    key_value_ref[1] = picked[:rows, 2 * cols : 3 * cols]
    out_ref[...] = picked[:rows, 3 * cols : 4 * cols]
    inner_ref[:, :hidden] = picked[:rows, 4 * cols :]
    inner_ref[:, hidden:] = picked[rows:, :hidden]
    down_ref[...] = picked[rows:, hidden:]


def unpack_layer(gathered, layer_idx, thin, features, cols, hidden):
    group = 8
    tall = 2 * thin * group
    flat = thin * group
    width = gathered.shape[1] // LAYERS
    blocks = features // flat
    spot = jnp.arange(tall, dtype=jnp.int32)
    half = spot // flat
    source = (spot % flat) // thin * (2 * thin) + half * thin + spot % thin
    order = (source[:, None] == jnp.arange(tall, dtype=jnp.int32)[None, :]).astype(jnp.bfloat16)
    return pl.pallas_call(
        unpack_kernel,
        grid=(2, blocks),
        in_specs=[
            pl.BlockSpec((tall, tall), lambda t, r: (0, 0)),
            pl.BlockSpec((tall, width), lambda t, r: (t * blocks + r, layer_idx)),
        ],
        out_specs=[
            pl.BlockSpec((flat, cols), lambda t, r: (r, t)),
            pl.BlockSpec((2, flat, cols), lambda t, r: (0, r, t)),
            pl.BlockSpec((flat, cols), lambda t, r: (r, t)),
            pl.BlockSpec((flat, hidden), lambda t, r: (r, t)),
            pl.BlockSpec((flat, hidden), lambda t, r: (r, t)),
        ],
        out_shape=[
            jax.ShapeDtypeStruct((features, 2 * cols), jnp.bfloat16),
            jax.ShapeDtypeStruct((2, features, 2 * cols), jnp.bfloat16),
            jax.ShapeDtypeStruct((features, 2 * cols), jnp.bfloat16),
            jax.ShapeDtypeStruct((features, 2 * hidden), jnp.bfloat16),
            jax.ShapeDtypeStruct((features, 2 * hidden), jnp.bfloat16),
        ],
        compiler_params=pltpu.CompilerParams(vmem_limit_bytes=40 * 1024 * 1024),
        name="unpack_layer",
    )(order, gathered)


def gather_weights(qkv_weight, out_weight, inner_weight, down_weight):
    layers = qkv_weight.shape[0]
    thin = qkv_weight.shape[3]
    cols, hidden = out_weight.shape[1], inner_weight.shape[1]
    piece = jnp.concatenate(
        [qkv_weight.reshape(layers, -1, thin), out_weight, inner_weight, down_weight], axis=1
    )
    width = piece.shape[1]
    piece = piece.reshape(layers, 2, width // 2, thin).transpose(1, 3, 0, 2).reshape(2 * thin, width)
    whole = lax.all_gather(piece, ALL, axis=0, tiled=True)
    features = whole.shape[0] // 4
    return [unpack_layer(whole, layer, thin, features, cols, hidden) for layer in range(layers)]


def coords(flat):
    dp = flat >> 1
    return [(flat & 1) * 2 + (dp >> 5), (dp >> 3) & 3, (dp >> 1) & 3, dp & 1]


def flat_index(x, z, y, core):
    return ((((x & 1) * 4 + z) * 4 + y) * 2 + core) * 2 + (x >> 1)


def partner(pos, kind):
    return pos ^ 1 if kind == 0 else (pos ^ 1) ^ 2


def exchange(values, axis, kind=0):
    pairs = []
    for flat in range(128):
        place = coords(flat)
        place[axis] = place[axis] ^ 1 if axis == 3 else partner(place[axis], kind)
        pairs.append((flat, flat_index(*place)))
    return lax.ppermute(values, ("dp", "tensor"), pairs)


def add_low(left, right):
    return (left.astype(jnp.float32) + right.astype(jnp.float32)).astype(jnp.bfloat16)


def pick(values, index, dim):
    return lax.dynamic_slice_in_dim(values, index, 1, dim)


def halve_first(values, place, axis, kind):
    me = place[axis]
    first, second = partner(me, kind), partner(me, 1 - kind)
    sent = jnp.concatenate(
        [pick(values, first, axis), pick(values, partner(first, 1 - kind), axis)], axis=axis
    )
    got = exchange(sent, axis, kind)
    kept = jnp.concatenate([pick(values, me, axis), pick(values, second, axis)], axis=axis)
    return add_low(kept, got)


def halve_second(kept, axis, kind):
    last = exchange(lax.slice_in_dim(kept, 1, 2, axis=axis), axis, 1 - kind)
    return add_low(lax.slice_in_dim(kept, 0, 1, axis=axis), last)


def scatter_rounds(parts, place, order):
    parts = [part.reshape(4, 4, 4, -1, part.shape[-1]) for part in parts]
    for step, axis in enumerate(order):
        if step == 1:
            parts = [jnp.concatenate(parts, axis=-1)]
        parts = yield [halve_first(part, place, axis, kind) for kind, part in enumerate(parts)]
        parts = yield [halve_second(part, axis, kind) for kind, part in enumerate(parts)]


def scatter_all(parts, place, order):
    rounds = scatter_rounds(parts, place, order)
    parts = next(rounds)
    for _ in range(2 * len(order) - 1):
        parts = rounds.send(parts)
    return parts[0].reshape(-1, parts[0].shape[-1])


def lane_halves(values):
    half = values.shape[-1] // 2
    return [values[..., :half], values[..., half:]]


def sum_all(values):
    values = values + exchange(values, 3)
    for axis in range(3):
        for kind in range(2):
            values = values + exchange(values, axis, kind)
    return values


def pack_kernel(*refs):
    packed = refs[-1]
    row = 0
    for ref in refs[:-1]:
        for part in range(ref.shape[1] // packed.shape[1]):
            packed[row : row + 1, :] = ref[:, part * packed.shape[1] : (part + 1) * packed.shape[1]]
            row += 1


def pack_rows(vectors, features):
    rows = sum(vector.shape[1] for vector in vectors) // features
    return pl.pallas_call(
        pack_kernel,
        out_shape=jax.ShapeDtypeStruct((rows, features), jnp.float32),
        name="pack_rows",
    )(*vectors)


def row_major(matrix):
    return with_layout_constraint(matrix, Layout(major_to_minor=(0, 1)))


def column_parts(matrix, offset, width):
    step = matrix.shape[1] // 2
    return [lax.dynamic_slice_in_dim(matrix, t * step + offset, width, 1) for t in range(2)]


def grads_of(left, right, offset, width):
    return jnp.stack([row_major(tn(left, part).astype(jnp.bfloat16)) for part in column_parts(right, offset, width)])


def reduce_core(make, core):
    got = exchange(make(1 - core), 3)
    return add_low(make(core), got)


WINDOW = 32


def cut_kernel(cuts, place_ref, first_ref, *refs):
    summed, out, window, copied = refs[:6], refs[6], refs[7], refs[8]
    start = pl.multiple_of(place_ref[0], 16)
    copies = []
    for index, array in enumerate(summed):
        width = cuts[index + 1] - cuts[index]
        first_col = pl.multiple_of(place_ref[2] * width, 128)
        copies.append(
            pltpu.make_async_copy(
                array.at[pl.ds(start, WINDOW), pl.ds(first_col, width)],
                window.at[:, pl.ds(cuts[index], width)],
                copied.at[index],
            )
        )
        copies[-1].start()
    out[0] = first_ref[...].astype(jnp.float32)
    for copy in copies:
        copy.wait()
    rows = out.shape[1]
    row = jax.lax.broadcasted_iota(jnp.int32, (rows, WINDOW), 0)
    spot = jax.lax.broadcasted_iota(jnp.int32, (rows, WINDOW), 1)
    chosen = jnp.where(spot == row + place_ref[1], 1.0, 0.0).astype(jnp.bfloat16)
    out[1] = jnp.dot(chosen, window[...], preferred_element_type=jnp.float32)


def cut_rows(first_own, summed, dp_idx, tensor_idx, thin):
    features = summed[0].shape[0]
    start = jnp.minimum(dp_idx * thin // 16 * 16, features - WINDOW)
    place = jnp.stack([start, dp_idx * thin - start, tensor_idx]).astype(jnp.int32)
    cuts = [0]
    for array in summed:
        cuts.append(cuts[-1] + array.shape[1] // 2)
    vmem = pl.BlockSpec(memory_space=pltpu.VMEM)
    return pl.pallas_call(
        functools.partial(cut_kernel, tuple(cuts)),
        in_specs=[pl.BlockSpec(memory_space=pltpu.SMEM), vmem] + [pl.BlockSpec(memory_space=pltpu.HBM)] * 6,
        out_specs=vmem,
        out_shape=jax.ShapeDtypeStruct((LAYERS, 16, cuts[-1]), jnp.float32),
        scratch_shapes=[pltpu.VMEM((WINDOW, cuts[-1]), jnp.bfloat16), pltpu.SemaphoreType.DMA((6,))],
        compiler_params=pltpu.CompilerParams(vmem_limit_bytes=56 * 1024 * 1024),
        name="cut_rows",
    )(place, jnp.pad(first_own, ((0, 16 - thin), (0, 0))), *summed)


def split_heads(matrix):
    return matrix.reshape(matrix.shape[0], -1, HEAD).transpose(1, 0, 2)


def join_heads(matrix):
    return matrix.transpose(1, 0, 2).reshape(matrix.shape[1], -1)


def body(
    tokens,
    doc_lengths,
    qkv_weight,
    out_weight,
    inner_weight,
    down_weight,
    query_value_bias,
    hidden_bias,
    shifts,
    gains,
    cotangent,
):
    half_len, features = tokens.shape[1:]
    thin = qkv_weight.shape[3]
    head_cols = qkv_weight.shape[2]
    hidden_cols = inner_weight.shape[1]
    scale_factor = 1.0 / math.sqrt(HEAD)
    tensor_idx = lax.axis_index("tensor")
    dp_idx = lax.axis_index("dp")
    core = dp_idx & 1
    place = [tensor_idx * 2 + (dp_idx >> 5), (dp_idx >> 3) & 3, (dp_idx >> 1) & 3]

    weights = gather_weights(qkv_weight, out_weight, inner_weight, down_weight)
    bias_rows = jnp.concatenate(
        [query_value_bias.reshape(2 * LAYERS, head_cols), hidden_bias.reshape(-1, head_cols)], axis=0
    )
    bias_all = lax.all_gather(bias_rows, "tensor", axis=0, tiled=False)
    qv_bias = bias_all[:, : 2 * LAYERS].reshape(2, LAYERS, 2, head_cols)
    qv_bias = qv_bias.transpose(1, 2, 0, 3).reshape(LAYERS, 2, 2 * head_cols)
    hidden_full = bias_all[:, 2 * LAYERS :].reshape(2, LAYERS, hidden_cols)
    hidden_full = hidden_full.transpose(1, 0, 2).reshape(LAYERS, 2 * hidden_cols)

    position = jnp.arange(half_len, dtype=jnp.int32)
    mine_pos = position + tensor_idx * half_len
    key_pos = jnp.concatenate([mine_pos, position + (1 - tensor_idx) * half_len])
    first_end = doc_lengths[0, 0]
    second_end = first_end + doc_lengths[0, 1]

    def segment(pos):
        return (pos >= first_end).astype(jnp.int32) + (pos >= second_end).astype(jnp.int32)

    same_doc = segment(mine_pos)[:, None] == segment(key_pos)[None, :]

    hidden_state = tokens[0].astype(jnp.float32)
    rounded = tokens[0]
    saved_acts = []
    for layer_idx in range(LAYERS):
        query_w, key_value_w, out_w, inner_w, down_w = weights[layer_idx]
        rows = jnp.concatenate([rounded, swap_halves(rounded)], axis=0)
        query_b = (nn(rounded, query_w) + qv_bias[layer_idx, 0]).astype(jnp.bfloat16)
        key_b = nn(rows, key_value_w[0]).astype(jnp.bfloat16)
        value_b = (nn(rows, key_value_w[1]) + qv_bias[layer_idx, 1]).astype(jnp.bfloat16)
        query_h, key_h, value_h = split_heads(query_b), split_heads(key_b), split_heads(value_b)
        scores = (
            jnp.einsum("hqd,hkd->hqk", query_h, key_h, preferred_element_type=jnp.float32) * scale_factor
        )
        scores = jnp.where(same_doc[None], scores, masked_value)
        row_max = jnp.max(scores, axis=-1, keepdims=True)
        raised = jnp.exp(scores - row_max)
        row_total = jnp.sum(raised, axis=-1, keepdims=True)
        attn_probs = (raised / row_total).astype(jnp.bfloat16)
        log_total = row_max + jnp.log(row_total)
        attended = jnp.einsum("hqk,hkd->hqd", attn_probs, value_h, preferred_element_type=jnp.float32)
        attended_b = join_heads(attended.astype(jnp.bfloat16))
        branch = nt(attended_b, out_w)
        normed, normal_one, inverse_one = layer_norm(
            hidden_state + branch + shifts[layer_idx, 0], gains[layer_idx, 0], shifts[layer_idx, 1]
        )
        normed_low = normed.astype(jnp.bfloat16)
        pre_act = nn(normed_low, inner_w) + hidden_full[layer_idx]
        activated_b = exact_gelu(pre_act).astype(jnp.bfloat16)
        mlp_out = nt(activated_b, down_w)
        hidden_state, normal_two, inverse_two = layer_norm(
            normed + mlp_out + shifts[layer_idx, 2], gains[layer_idx, 1], shifts[layer_idx, 3]
        )
        saved_acts.append(
            (rows, query_h, key_h, value_h, log_total, attended_b, normal_one, inverse_one, normed_low,
             pre_act, activated_b, normal_two, inverse_two)
        )
        rounded = hidden_state.astype(jnp.bfloat16)
    output = hidden_state

    def backward(layer_idx, state_grad):
        query_w, key_value_w, out_w, inner_w, down_w = weights[layer_idx]
        (rows, query_h, key_h, value_h, log_total, attended_b, normal_one, inverse_one, normed_low,
         pre_act, activated_b, normal_two, inverse_two) = saved_acts[layer_idx]
        pre_two_grad = norm_back(state_grad, normal_two, inverse_two, gains[layer_idx, 1])
        gain_two = jnp.sum(state_grad * normal_two, axis=0, keepdims=True)
        beta_two = jnp.sum(state_grad, axis=0, keepdims=True)
        shift_two = jnp.sum(pre_two_grad, axis=0, keepdims=True)
        mlp_grad_b = pre_two_grad.astype(jnp.bfloat16)
        half_hidden = hidden_cols // 2
        if layer_idx > 0:
            down_local = tn(mlp_grad_b, activated_b).astype(jnp.bfloat16)
        else:
            down_part = reduce_core(
                lambda side: grads_of(mlp_grad_b, activated_b, side * half_hidden, half_hidden), core
            )
        activated_grad = nn(mlp_grad_b, down_w)
        _, gelu_back = jax.vjp(exact_gelu, pre_act)
        pre_act_grad = gelu_back(activated_grad)[0].astype(jnp.bfloat16)
        hidden_part = jnp.sum(pre_act_grad.astype(jnp.float32), axis=0, keepdims=True)
        if layer_idx > 0:
            inner_local = tn(normed_low, pre_act_grad).astype(jnp.bfloat16)
        else:
            inner_part = reduce_core(
                lambda side: grads_of(normed_low, pre_act_grad, side * half_hidden, half_hidden), core
            )
            wide_parts = [inner_part, down_part]
        normed_grad = pre_two_grad + nt(pre_act_grad, inner_w)
        pre_one_grad = norm_back(normed_grad, normal_one, inverse_one, gains[layer_idx, 0])
        gain_one = jnp.sum(normed_grad * normal_one, axis=0, keepdims=True)
        beta_one = jnp.sum(normed_grad, axis=0, keepdims=True)
        shift_one = jnp.sum(pre_one_grad, axis=0, keepdims=True)
        attn_grad_b = pre_one_grad.astype(jnp.bfloat16)
        if layer_idx > 0:
            out_local = tn(attn_grad_b, attended_b).astype(jnp.bfloat16)
        attended_grad = nn(attn_grad_b, out_w).astype(jnp.bfloat16)
        attended_grad_h = split_heads(attended_grad)
        scores = (
            jnp.einsum("hqd,hkd->hqk", query_h, key_h, preferred_element_type=jnp.float32) * scale_factor
        )
        scores = jnp.where(same_doc[None], scores, masked_value)
        probs_full = jnp.exp(scores - log_total)
        probs_low = probs_full.astype(jnp.bfloat16)
        value_grad = jnp.einsum("hqk,hqd->hkd", probs_low, attended_grad_h, preferred_element_type=jnp.float32)
        prob_grad = jnp.einsum("hqd,hkd->hqk", attended_grad_h, value_h, preferred_element_type=jnp.float32)
        row_dot = jnp.sum(prob_grad * probs_full, axis=-1, keepdims=True)
        score_grad = (probs_full * (prob_grad - row_dot)).astype(jnp.bfloat16)
        query_grad = (
            jnp.einsum("hqk,hkd->hqd", score_grad, key_h, preferred_element_type=jnp.float32) * scale_factor
        )
        key_grad = (
            jnp.einsum("hqk,hqd->hkd", score_grad, query_h, preferred_element_type=jnp.float32) * scale_factor
        )
        query_grad_b = join_heads(query_grad.astype(jnp.bfloat16))
        key_grad_b = join_heads(key_grad.astype(jnp.bfloat16))
        value_grad_b = join_heads(value_grad.astype(jnp.bfloat16))
        qv_part = [
            jnp.sum(query_grad_b.astype(jnp.float32), axis=0, keepdims=True),
            jnp.sum(value_grad_b.astype(jnp.float32), axis=0, keepdims=True),
        ]
        if layer_idx > 0:
            query_local = tn(rows[:half_len], query_grad_b).astype(jnp.bfloat16)
            key_local = tn(rows, key_grad_b).astype(jnp.bfloat16)
            value_local = tn(rows, value_grad_b).astype(jnp.bfloat16)
            locals_all = tuple(
                row_major(part)
                for part in (query_local, key_local, value_local, out_local, inner_local, down_local)
            )
        else:
            padding = ((0, half_len), (0, 0))
            query_pad, attn_pad, attended_pad = (
                jnp.pad(v, padding) for v in (query_grad_b, attn_grad_b, attended_b)
            )

            def first_grads(side):
                return grads_of(rows, jnp.where(side == 0, query_pad, value_grad_b), 0, head_cols)

            def second_grads(side):
                left = jnp.where(side == 0, rows, attn_pad)
                return grads_of(left, jnp.where(side == 0, key_grad_b, attended_pad), 0, head_cols)

            attn_parts = [reduce_core(first_grads, core), reduce_core(second_grads, core)]
        both = nt(key_grad_b, key_value_w[0]) + nt(value_grad_b, key_value_w[1])
        theirs = swap_halves(both[half_len:].astype(jnp.bfloat16))
        state_grad = (
            pre_one_grad
            + nt(query_grad_b, query_w)
            + both[:half_len]
            + theirs.astype(jnp.float32)
        )
        sums = [shift_one, beta_one, shift_two, beta_two, gain_one, gain_two, *qv_part, hidden_part]
        if layer_idx > 0:
            return state_grad, sums, locals_all
        return state_grad, sums, (wide_parts, attn_parts)

    second_grad, second_sums, second_parts = backward(1, cotangent[0])
    second_parts, second_grad = lax.optimization_barrier((second_parts, second_grad))
    summed = lax.psum(second_parts, ALL)

    def first_layer(state_grad, second_sums):
        state_grad, sums, (wide_parts, attn_parts) = backward(0, state_grad)
        small, attn_parts = lax.optimization_barrier((pack_rows(sums + second_sums, features), attn_parts))
        small = sum_all(small)
        inner_part, down_part = wide_parts
        groups = (
            scatter_all(attn_parts, place, (0, 1, 2)),
            scatter_all(lane_halves(inner_part), place, (1, 2, 0)),
            scatter_all(lane_halves(down_part), place, (2, 0, 1)),
        )
        first_rows = jnp.concatenate(groups, axis=1)
        theirs = exchange(lax.dynamic_slice_in_dim(first_rows, (1 - core) * thin, thin, 0), 3)
        mine = lax.dynamic_slice_in_dim(first_rows, core * thin, thin, 0)
        low_side = jnp.where(core == 0, mine, theirs).reshape(thin, 3, -1)
        high_side = jnp.where(core == 0, theirs, mine).reshape(thin, 3, -1)
        first_own = jnp.concatenate([low_side, high_side], axis=2).reshape(thin, -1)
        return state_grad, first_own, small

    def no_layer(state_grad, second_sums):
        first_own = jnp.zeros((thin, 4 * head_cols + 2 * hidden_cols), jnp.bfloat16)
        return state_grad, first_own, jnp.zeros((LAYERS * 12, features), jnp.float32)

    state_grad, first_own, small = lax.cond(
        doc_lengths[0, 0] >= 0, first_layer, no_layer, second_grad, second_sums
    )
    small_sum = small.reshape(LAYERS, -1)
    both_own = cut_rows(first_own, summed, dp_idx, tensor_idx, thin)[:, :thin]

    def result(start, stop):
        return both_own[:, :, start:stop].transpose(0, 2, 1)

    qkv_result = both_own[:, :, : 3 * head_cols].reshape(LAYERS, thin, 3, head_cols).transpose(0, 2, 3, 1)
    out_result = result(3 * head_cols, 4 * head_cols)
    inner_result = result(4 * head_cols, 4 * head_cols + hidden_cols)
    down_result = result(4 * head_cols + hidden_cols, 4 * head_cols + 2 * hidden_cols)
    shift_total = small_sum[:, : 4 * features].reshape(LAYERS, 4, features)
    gain_total = small_sum[:, 4 * features : 6 * features].reshape(LAYERS, 2, features)
    qv_total = lax.dynamic_slice_in_dim(
        small_sum[:, 6 * features : 8 * features].reshape(LAYERS, 2, features), tensor_idx * head_cols, head_cols, 2
    )
    hidden_total = lax.dynamic_slice_in_dim(small_sum[:, 8 * features :], tensor_idx * hidden_cols, hidden_cols, 1)
    return (
        output[None],
        state_grad[None],
        qkv_result,
        out_result,
        inner_result,
        down_result,
        qv_total,
        hidden_total,
        shift_total,
        gain_total,
    )


def solution(mesh):
    in_specs = (
        P("dp", "tensor", None),
        P("dp", None),
        P(None, None, "tensor", "dp"),
        P(None, "tensor", "dp"),
        P(None, "tensor", "dp"),
        P(None, "tensor", "dp"),
        P(None, None, "tensor"),
        P(None, "tensor"),
        P(),
        P(),
        P("dp", "tensor", None),
    )
    out_specs = (
        P("dp", "tensor", None),
        P("dp", "tensor", None),
        P(None, None, "tensor", "dp"),
        P(None, "tensor", "dp"),
        P(None, "tensor", "dp"),
        P(None, "tensor", "dp"),
        P(None, None, "tensor"),
        P(None, "tensor"),
        P(),
        P(),
    )
    return jax.shard_map(body, mesh=mesh, in_specs=in_specs, out_specs=out_specs, check_vma=False)
```
